32 devices in a mesh: dp: 8 (over y, x, core), tensor: 4 (over z).
Axes of the slice: x: 2, y: 2, z: 4, core: 2. Of those that a mesh axis runs over, the one named last changes fastest.
Arguments:
- tokens: bfloat16 [16, 4096, 768], P('dp', 'tensor'), may hold values from -6 to 6, as said below
- w_in: bfloat16 [768, 3072], P(None, 'tensor'), may hold values from -0.21875 to 0.21875
- b_in: bfloat16 [3072], P('tensor'), may hold values from -3 to 3
- w_out: bfloat16 [3072, 768], P('tensor'), may hold values from -0.109375 to 0.109375
- b_out: float32 [768], replicated, may hold values from -3 to 3
- gain_one: float32 [768], replicated, may hold values from 0.1 to 1.9
- shift_one: float32 [768], replicated, may hold values from -3 to 3
- gain_two: float32 [768], replicated, may hold values from 0.1 to 1.9
- shift_two: float32 [768], replicated, may hold values from -3 to 3
- out_grad: float32 [16, 4096, 768], P('dp', 'tensor'), may hold values from -25 to 25, as said below
Outputs:
- activations: float32 [16, 4096, 768], P('dp', 'tensor')
- input_grad: float32 [16, 4096, 768], P('dp', 'tensor')
- grad_w_in: float32 [768, 3072], P(None, 'tensor')
- grad_b_in: float32 [3072], P('tensor')
- grad_w_out: float32 [3072, 768], P('tensor')
- grad_b_out: float32 [768], replicated
- grad_gain_one: float32 [768], replicated
- grad_shift_one: float32 [768], replicated
- grad_gain_two: float32 [768], replicated
- grad_shift_two: float32 [768], replicated
The draws below stay inside these ranges and needn't reach their ends.
Inputs may be any that keep to these rules, and one draw needn't show every extreme that they name: `tokens`: padding sequences (index 15 modulo 16, and the last one) are all zeros. `out_grad`: zero on every padding sequence (index 15 modulo 16, and the last one).
All inputs are finite; a program needn't handle non-finite values.
Results may differ from the reference program's by a relative error of at most 0.018.
Values may be sent and summed in bfloat16 or wider, within the bound.
No kernel may reach another device: no remote copies, remote signals or barrier semaphores. Data moves between devices by JAX's collectives and lax.ppermute only.
A program may use at most 384 MiB of HBM per device.

```python
import math
import jax
import jax.numpy as jnp
from jax import lax

D = 768
FF = 3072
P_SIZE = 64
L = 4096
SEQS = 16


def live_sequences():
    index = jnp.arange(SEQS, dtype=jnp.int32)
    padding = (index % 16 == 15) | (index == SEQS - 1)
    return jnp.where(padding, 0.0, 1.0).astype(jnp.float32)[:, None, None]


def draw_tokens(key, part):
    key = jax.random.fold_in(key, 5)
    base = jnp.clip(jax.random.normal(key, (SEQS, L, D)), -6.0, 6.0)
    return (live_sequences() * base).astype(jnp.bfloat16)


def draw_out_grad(key, part):
    key = jax.random.fold_in(key, 11)
    key_base, key_column = jax.random.split(key, 2)
    seq_pos = jnp.arange(SEQS, dtype=jnp.float32) / max(SEQS - 1, 1)
    row_pos = jnp.arange(L, dtype=jnp.float32) / max(L - 1, 1)
    scale = (1.0 + 2.0 * seq_pos)[:, None, None] * (1.0 + 2.0 * row_pos)[None, :, None] / 3.0
    column = jnp.exp(jax.random.uniform(key_column, (1, 1, D), minval=-0.69, maxval=0.69))
    base = jnp.clip(jax.random.normal(key_base, (SEQS, L, D)), -4.0, 4.0)
    return (live_sequences() * scale * column * base).astype(jnp.float32)


def block_levels(key, shape, shards, low, high):
    level = 1.0
    for axis_at, shards_of in shards:
        draws = jax.random.uniform(jax.random.fold_in(jax.random.fold_in(key, 6), axis_at), (shards_of,), jnp.float32, low / len(shards), high / len(shards))
        level = level * jnp.repeat(jnp.exp(draws), shape[axis_at] // shards_of).reshape((-1,) + (1,) * (len(shape) - 1 - axis_at))
    return level


def gaussian(own_key, shape, deviation, reach, cuts=(), kind=jnp.bfloat16):
    entries = jax.random.normal(own_key, shape, jnp.float32) * deviation
    if len(cuts) > 0:
        entries = block_levels(own_key, shape, cuts, -0.22, 0.18) * entries
    return jnp.clip(entries, min=-reach, max=reach).astype(kind)


def setup_inputs(seed: int = 0) -> dict:
    keys = jax.random.split(jax.random.key(seed), 11)
    return {
        "tokens": draw_tokens(jax.random.fold_in(keys[10], 71), 0),
        "w_in": gaussian(keys[1], (D, FF), D ** -0.5, 0.21875, ((1, 4),)),
        "b_in": gaussian(keys[2], (FF,), 0.5, 3.0, ((0, 4),)),
        "w_out": gaussian(keys[3], (FF, D), FF ** -0.5, 0.109375, ((0, 4),)),
        "b_out": gaussian(keys[4], (D,), 0.5, 3.0, (), jnp.float32),
        "gain_one": jnp.clip(1.0 + 0.18 * jax.random.normal(keys[5], (D,), jnp.float32), 0.1, 1.9),
        "shift_one": gaussian(keys[6], (D,), 0.5, 3.0, (), jnp.float32),
        "gain_two": jnp.clip(1.0 + 0.18 * jax.random.normal(keys[7], (D,), jnp.float32), 0.1, 1.9),
        "shift_two": gaussian(keys[8], (D,), 0.5, 3.0, (), jnp.float32),
        "out_grad": draw_out_grad(jax.random.fold_in(keys[10], 71), 0),
    }


@jax.custom_vjp
def low(v):
    return lax.optimization_barrier(v.astype(jnp.bfloat16)).astype(jnp.float32)

@jax.custom_vjp
def low_back(v):
    return v

def low_keep(v):
    return (low(v), None)

def low_pass(kept, grad):
    return (grad,)

def back_keep(v):
    return (v, None)

def back_low(kept, grad):
    return (low(grad),)
low.defvjp(low_keep, low_pass)
low_back.defvjp(back_keep, back_low)
epsilon = 1e-12

def wave_tables(width):
    index = jnp.arange(width, dtype=jnp.int32)
    angle = 2.0 * math.pi / width * (index[:, None] * index[None, :] % width).astype(jnp.float32)
    return (low(jnp.cos(angle)), low(jnp.sin(angle)))

def twiddles(order):
    index = jnp.arange(order, dtype=jnp.int32)
    angle = 2.0 * math.pi / (order * order) * (index[:, None] * index[None, :]).astype(jnp.float32)
    return (jnp.cos(angle)[:, :, None], jnp.sin(angle)[:, :, None])

def matmul(left, right):
    return jnp.dot(left, right, precision=lax.Precision.HIGHEST, preferred_element_type=jnp.float32)

def einsum_high(form, left, right):
    return jnp.einsum(form, left, right, precision=lax.Precision.HIGHEST, preferred_element_type=jnp.float32)

def layer_norm(resid, gain, shift):
    centered = resid - lax.optimization_barrier(jnp.mean(resid, axis=-1, keepdims=True))
    scaled = centered * lax.rsqrt(lax.optimization_barrier(jnp.mean(centered * centered, axis=-1, keepdims=True)) + epsilon)
    return scaled * gain + shift

def make_forward():
    cos_width, sin_width = wave_tables(D)
    cos_fac, sin_fac = wave_tables(P_SIZE)
    turn_cos, turn_sin = twiddles(P_SIZE)

    def forward(seq, w_in, b_in, w_out, b_out, gain_one, shift_one, gain_two, shift_two):
        wave_a = low_back(low(matmul(seq, cos_width))).reshape(P_SIZE, P_SIZE, D)
        wave_b = low_back(low(matmul(seq, sin_width))).reshape(P_SIZE, P_SIZE, D)
        section_real = low_back(einsum_high('kn,nmd->kmd', cos_fac, wave_a) - einsum_high('kn,nmd->kmd', sin_fac, wave_b))
        section_quad = low_back(einsum_high('kn,nmd->kmd', cos_fac, wave_b) + einsum_high('kn,nmd->kmd', sin_fac, wave_a))
        turn_real = low_back(low(turn_cos * section_real - turn_sin * section_quad))
        turn_imag = low_back(low(turn_cos * section_quad + turn_sin * section_real))
        mixed = einsum_high('bn,anj->baj', cos_fac, turn_real) - einsum_high('bn,anj->baj', sin_fac, turn_imag)
        mixed = low_back(mixed.reshape(L, D))
        normed_one = layer_norm(seq + mixed, gain_one, shift_one)
        pre_act = low_back(matmul(low(normed_one), w_in) + b_in)
        hidden = low(jax.nn.gelu(pre_act, approximate=True))
        branch = low_back(matmul(hidden, w_out) + b_out)
        return layer_norm(normed_one + branch, gain_two, shift_two)
    return forward

def reference(tokens, w_in, b_in, w_out, b_out, gain_one, shift_one, gain_two, shift_two, out_grad):
    forward = make_forward()
    params = (w_in.astype(jnp.float32), b_in.astype(jnp.float32), w_out.astype(jnp.float32), b_out, gain_one, shift_one, gain_two, shift_two)

    def one_sequence(totals, item):
        seq, cotangent = item
        result, pull = jax.vjp(forward, seq.astype(jnp.float32), *params)
        grads = pull(cotangent)
        totals = tuple((total + grad for total, grad in zip(totals, grads[1:])))
        return (totals, (result, grads[0]))
    zeros = tuple((jnp.zeros_like(param) for param in params))
    totals, (results, input_grad) = lax.scan(one_sequence, zeros, (tokens, out_grad))
    return (results, input_grad, totals[0], totals[1], totals[2], totals[3], totals[4], totals[5], totals[6], totals[7])
```

```python
import functools
import math

import jax
import jax.numpy as jnp
import numpy as np
from jax import lax
from jax.experimental import pallas as pl
from jax.experimental.pallas import tpu as pltpu
from jax.sharding import PartitionSpec as P

epsilon = 1e-12
LOW = jnp.bfloat16
F32 = jnp.float32
BOTH = ("dp", "tensor")
SORTED = 256
VMEM_BYTES = 60 * 1024 * 1024
LONG = pl.CostEstimate(flops=3 * 10**11, bytes_accessed=1 << 20, transcendentals=0)
LIGHT = pl.CostEstimate(flops=1024, bytes_accessed=1024, transcendentals=0)
GELU_C = math.sqrt(2.0 / math.pi)
GELU_A = 0.044715


def dot(left, right):
    return lax.dot_general(left, right, (((1,), (0,)), ((), ())), preferred_element_type=F32)


def dot_nt(left, right):
    return lax.dot_general(left, right, (((1,), (1,)), ((), ())), preferred_element_type=F32)


class Plan:
    def __init__(self, mesh, seqs):
        self.dp = mesh.shape["dp"]
        self.parts = mesh.shape["tensor"]
        self.seqs = seqs
        self.group = self.parts // seqs
        self.span = self.group // 2
        assert seqs == 2 and self.group >= 2 and self.parts & (self.parts - 1) == 0
        assert self.dp & (self.dp - 1) == 0
        self.pairs = [(0, self.group)] + [(g, self.parts - g) for g in range(1, self.group)]

    def flat(self, d, t):
        return d * self.parts + t

    def owner(self, core, block):
        seq, g = divmod(block, self.group)
        return g % 2, (core * self.seqs + seq) * self.span + g // 2

    def out_perm(self, r):
        perm = []
        for d in range(self.dp):
            for t in range(self.parts):
                core, chip = self.owner(d % 2, t ^ r)
                perm.append((self.flat(d, t), self.flat(d - d % 2 + core, chip)))
        return perm

    def back_perm(self, r):
        return [(dst, src) for src, dst in self.out_perm(r)]

    def group_perm(self, j):
        perm = []
        for d in range(self.dp):
            for t in range(self.parts):
                g = ((t % self.span) * 2 + d % 2) ^ j
                other = self.flat(d - d % 2 + g % 2, t - t % self.span + g // 2)
                perm.append((self.flat(d, t), other))
        return perm

    def xor_perm(self, dp_bits, z_bits):
        return [
            (self.flat(d, t), self.flat(d ^ dp_bits, t ^ z_bits))
            for d in range(self.dp)
            for t in range(self.parts)
        ]

    def fold_table(self):
        table = np.zeros((self.group, 2, self.parts), np.float32)
        for g in range(self.group):
            for q in range(self.parts):
                if g == 0:
                    table[g, :, q] = (1.0, (-1.0) ** q)
                else:
                    angle = 2.0 * math.pi * (q * g % self.parts) / self.parts
                    pair = (math.cos(angle), -math.sin(angle))
                    table[g, :, q] = [0.0 if abs(v) < 1e-9 else v for v in pair]
        return table


def whole(shape):
    return pl.BlockSpec(shape, lambda *_: (0,) * len(shape))


def once(shape):
    return pl.BlockSpec(shape, lambda *_: (0,) * len(shape), pipeline_mode=pl.Buffered(1))


SCALARS = pl.BlockSpec(memory_space=pltpu.SMEM)
LATER = pl.BlockSpec(memory_space=pl.ANY)


def params():
    return pltpu.CompilerParams(vmem_limit_bytes=VMEM_BYTES)


def block_order(plan, size):
    per = size // plan.parts
    return np.array([plan.parts * i + ka for pair in plan.pairs for ka in pair for i in range(per)])


def sort_kernel(plan, where, perm, value, *refs):
    outs = refs[-plan.parts :]
    per = perm.shape[0] // plan.parts
    for s in range(plan.seqs):
        rows = dot(perm[...], value[s].astype(LOW)).astype(LOW)
        for g in range(plan.group):
            piece = rows[g * 2 * per : (g + 1) * 2 * per].reshape(2, per, rows.shape[-1])
            r = (s * plan.group + g) ^ where[0]
            for k, out in enumerate(outs):

                @pl.when(r == k)
                def _(out=out, piece=piece):
                    out[...] = piece


def sort_rows(plan, where, value, after=()):
    seqs, rows, width = value.shape
    size = min(SORTED, rows)
    per = size // plan.parts
    order = block_order(plan, size)
    perm = jnp.asarray(order[:, None] == np.arange(size)[None, :], LOW)
    shape = jax.ShapeDtypeStruct((2, rows // plan.parts, width), LOW)
    return pl.pallas_call(
        functools.partial(sort_kernel, plan),
        grid=(rows // size,),
        in_specs=[SCALARS, whole((size, size)), pl.BlockSpec((seqs, size, width), lambda b: (0, b, 0))]
        + [LATER] * len(after),
        out_specs=[pl.BlockSpec((2, per, width), lambda b: (0, b, 0))] * plan.parts,
        out_shape=[shape] * plan.parts,
        compiler_params=params(),
        cost_estimate=LIGHT,
        name="sort_rows",
    )(where, perm, value, *after)


def unsorter(plan, size):
    return jnp.asarray(np.arange(size)[:, None] == block_order(plan, size)[None, :], LOW)


def unsort_kernel(plan, where, perm, *refs):
    blocks, out, rows = refs[: plan.parts], refs[-2], refs[-1]
    per = perm.shape[0] // plan.parts
    for s in range(plan.seqs):
        for g in range(plan.group):
            r = (s * plan.group + g) ^ where[0]
            for k, block in enumerate(blocks):

                @pl.when(r == k)
                def _(block=block, g=g):
                    rows[g * 2 * per : (g + 1) * 2 * per] = block[...].reshape(2 * per, rows.shape[-1])

        out[s] = dot(perm[...], rows[...])


def unsort_rows(plan, where, blocks):
    _, per_rows, width = blocks[0].shape
    rows = per_rows * plan.parts
    size = min(SORTED, rows)
    per = size // plan.parts
    perm = unsorter(plan, size)
    return pl.pallas_call(
        functools.partial(unsort_kernel, plan),
        grid=(rows // size,),
        in_specs=[SCALARS, whole((size, size))]
        + [pl.BlockSpec((2, per, width), lambda b: (0, b, 0))] * plan.parts,
        out_specs=pl.BlockSpec((plan.seqs, size, width), lambda b: (0, b, 0)),
        out_shape=jax.ShapeDtypeStruct((plan.seqs, rows, width), F32),
        scratch_shapes=[pltpu.VMEM((size, width), LOW)],
        compiler_params=params(),
        cost_estimate=LIGHT,
        name="unsort_rows",
    )(where, perm, *blocks)


def fold_kernel(plan, stacked, where, factors, *refs):
    parts, group = plan.parts, plan.group
    if stacked:
        source, outs = refs[0], refs[-group:]
        terms = [source[0, r].astype(F32) for r in range(parts)]
    else:
        terms = [ref[0].astype(F32) for ref in refs[:parts]]
        outs, kept = refs[-1 - group : -1], refs[-1]
        for r in range(parts):
            kept[0, r] = refs[r][0]
    for j in range(group):
        for which in range(2):
            total = None
            for r in range(parts):
                place = ((where[2] ^ j) * 2 + which) * parts + (where[1] ^ r)
                term = factors[place] * terms[r]
                total = term if total is None else total + term
            outs[j][which] = total.astype(LOW)


def fold(plan, where, value, after=(), cost=LIGHT):
    stacked = not isinstance(value, (list, tuple))
    parts = plan.parts
    per, width = value.shape[2:] if stacked else value[0].shape[1:]
    step = min(256, per)
    steps = per // step
    factors = jnp.asarray(plan.fold_table().reshape(-1))
    stack = pl.BlockSpec((1, parts, step, width), lambda c, k: (c, 0, k, 0))
    single = pl.BlockSpec((1, step, width), lambda c, k: (c, k, 0))
    out = pl.BlockSpec((2, step, width), lambda c, k: (0, c * steps + k, 0))
    sums = jax.ShapeDtypeStruct((2, 2 * per, width), LOW)
    whole_shape = jax.ShapeDtypeStruct((2, parts, per, width), LOW)
    return pl.pallas_call(
        functools.partial(fold_kernel, plan, stacked),
        grid=(2, steps),
        in_specs=[SCALARS, SCALARS] + ([stack] if stacked else [single] * parts) + [LATER] * len(after),
        out_specs=[out] * plan.group + ([] if stacked else [stack]),
        out_shape=[sums] * plan.group + ([] if stacked else [whole_shape]),
        compiler_params=params(),
        cost_estimate=cost,
        name="fold_parts",
    )(where, factors, *([value] if stacked else value), *after)


def turn_waves(plan, where, pairs, wave, turned, step):
    first = jnp.where(where[2] == 0, 1.0, 0.0).astype(F32)
    rest = 1.0 - first
    width = wave.shape[0]
    own = pairs[0].shape[1]
    rows = own * plan.group
    for j, pair in enumerate(pairs):
        for k in range(own // step):
            span = slice(k * step, (k + 1) * step)
            pw = dot(pair[0, span], wave[...])
            qw = dot(pair[1, span], wave[...])
            pc, ps, qc, qs = pw[:, :width], pw[:, width:], qw[:, :width], qw[:, width:]
            at = j * own + k * step
            turned[0, at : at + step] = (pc + rest * qs).astype(LOW)
            turned[0, rows + at : rows + at + step] = (rest * qc - ps).astype(LOW)
            turned[1, at : at + step] = (first * qc + rest * (pc - qs)).astype(LOW)
            turned[1, rows + at : rows + at + step] = (-first * qs - rest * (qc + ps)).astype(LOW)


def normed(resid, gain, shift):
    centered = resid - jnp.mean(resid, axis=-1, keepdims=True)
    inverse = lax.rsqrt(jnp.mean(centered * centered, axis=-1, keepdims=True) + epsilon)
    scaled = centered * inverse
    return scaled * gain + shift, scaled, inverse


def forward_kernel(plan, where, *refs):
    group, parts = plan.group, plan.parts
    pairs, refs = refs[:group], refs[group:]
    (wave, cos_rows, sin_rows, taken, b_in, vectors, *refs) = refs
    (w_in, w_out), refs = split_weights(plan, refs)
    acts, (low_out, one_out, two_out, scales, hidden_out, slope_out, turned) = refs[:parts], refs[parts:]
    c, r = pl.program_id(0), pl.program_id(1)
    _, many, per, width = taken.shape
    rows = many * per

    @pl.when((c == 0) & (r == 0))
    def _():
        turn_waves(plan, where, pairs, wave, turned, min(256, pairs[0].shape[1]))

    mixed = section(cos_rows, sin_rows, turned, c)
    b_out, gain_one, shift_one, gain_two, shift_two = (vectors[k : k + 1] for k in range(5))
    resid = taken[0].reshape(rows, width).astype(F32) + mixed
    normed_one, scaled_one, inverse_one = normed(resid, gain_one, shift_one)
    low = normed_one.astype(LOW)
    low_out[0] = low.reshape(many, per, width)
    one_out[0] = scaled_one.astype(LOW).reshape(many, per, width)
    branch = normed_one + b_out
    for h in range(parts):
        pre = dot(low, w_in[h]) + b_in[h : h + 1]
        square = pre * pre
        bend = jnp.tanh(pre * (GELU_C + (GELU_C * GELU_A) * square))
        half = 0.5 * pre
        hidden = (half + half * bend).astype(LOW)
        slope = 0.5 + 0.5 * bend + half * (1.0 - bend * bend) * (GELU_C + (3.0 * GELU_C * GELU_A) * square)
        hidden_out[0, :, h] = hidden.reshape(many, per, hidden.shape[1])
        slope_out[0, :, h] = slope.astype(LOW).reshape(many, per, hidden.shape[1])
        branch = branch + dot(hidden, w_out[h])
    normed_two, scaled_two, inverse_two = normed(branch, gain_two, shift_two)
    two_out[0] = scaled_two.astype(LOW).reshape(many, per, width)
    lanes = lax.broadcasted_iota(jnp.int32, (rows, 128), 1)
    scales[0] = jnp.where(lanes == 0, inverse_one, inverse_two).reshape(many, per, 128)
    act = normed_two.astype(LOW)
    for k in range(parts):

        @pl.when(r == k // many)
        def _(k=k):
            acts[k][0] = act[k % many * per : (k % many + 1) * per]


def section(cos_rows, sin_rows, turned, c):
    rows = cos_rows.shape[2]
    return dot(cos_rows[0], turned[c, :rows]) + dot(sin_rows[0], turned[c, rows:])


def split_weights(plan, refs):
    if refs[0].shape[0] == 2 * plan.parts:
        return (refs[0].at[: plan.parts], refs[0].at[plan.parts :]), refs[1:]
    return refs[:2], refs[2:]


def forward(plan, where, pairs, wave, tables, taken, b_in, vectors, weights):
    parts = plan.parts
    _, _, per, width = taken.shape
    rows = per * parts
    hid = b_in.shape[1]
    many = 1
    tile = pl.BlockSpec((1, many, per, width), lambda c, r: (c, r, 0, 0))
    wide = pl.BlockSpec((1, many, parts, per, hid), lambda c, r: (c, r, 0, 0, 0))
    low = jax.ShapeDtypeStruct((2, parts, per, width), LOW)
    big = jax.ShapeDtypeStruct((2, parts, parts, per, hid), LOW)
    return pl.pallas_call(
        functools.partial(forward_kernel, plan),
        grid=(2, parts // many),
        in_specs=[SCALARS]
        + [once(pairs[0].shape)] * plan.group
        + [
            once(wave.shape),
            pl.BlockSpec((1, many * per, rows), lambda c, r: (c, r, 0)),
            pl.BlockSpec((1, many * per, rows), lambda c, r: (c, r, 0)),
            tile,
            once(b_in.shape),
            once(vectors.shape),
        ]
        + [once(w.shape) for w in weights],
        out_specs=[pl.BlockSpec((1, per, width), lambda c, r: (c, 0, 0))] * parts
        + [tile, tile, tile, pl.BlockSpec((1, many, per, 128), lambda c, r: (c, r, 0, 0)), wide, wide],
        out_shape=[jax.ShapeDtypeStruct((2, per, width), LOW)] * parts
        + [low, low, low, jax.ShapeDtypeStruct((2, parts, per, 128), F32), big, big],
        scratch_shapes=[pltpu.VMEM((2, 2 * rows, width), LOW)],
        compiler_params=params(),
        cost_estimate=LIGHT,
        name="mix_forward",
    )(where, *pairs, wave, *tables, taken, b_in, vectors, *weights)


def norm_back(grad, scaled, inverse, gain):
    grad_scaled = grad * gain
    return inverse * (
        grad_scaled
        - jnp.mean(grad_scaled, axis=-1, keepdims=True)
        - scaled * jnp.mean(grad_scaled * scaled, axis=-1, keepdims=True)
    )


def column_sum(value):
    return jnp.sum(value, axis=0, keepdims=True)


def backward_kernel(plan, core, *refs):
    parts = plan.parts
    cotangents, refs = refs[:parts], refs[parts:]
    (low, one, two, scales, hidden, slope, vectors, *refs) = refs
    (w_in, w_out), refs = split_weights(plan, refs)
    (first_out, mixed_out, sums, bias, *halves, grad_in, grad_out, cotangent) = refs
    c, r = pl.program_id(0), pl.program_id(1)
    step = c * parts + r

    for k in range(parts):

        @pl.when(r == k)
        def _(k=k):
            cotangent[...] = cotangents[k][0]

    @pl.when(step == 0)
    def _():
        sums[...] = jnp.zeros_like(sums)
        bias[...] = jnp.zeros_like(bias)
        grad_in[...] = jnp.zeros_like(grad_in)
        grad_out[...] = jnp.zeros_like(grad_out)

    gain_one, gain_two = vectors[1:2], vectors[3:4]
    inverse_one, inverse_two = scales[0, 0, :, 0:1], scales[0, 0, :, 1:2]
    grad = cotangent[...].astype(F32)
    scaled_two = two[0, 0].astype(F32)
    second = norm_back(grad, scaled_two, inverse_two, gain_two)
    branch = second.astype(LOW)
    sums[2:3] += column_sum(grad * scaled_two)
    sums[3:4] += column_sum(grad)
    sums[4:5] += column_sum(branch.astype(F32))
    low_turned = low[0, 0].T
    branch_turned = branch.T
    back = second
    for h in range(parts):
        pre = (dot_nt(branch, w_out[h]) * slope[0, 0, h].astype(F32)).astype(LOW)
        bias[h : h + 1] += column_sum(pre.astype(F32))
        back = back + dot_nt(pre, w_in[h])
        grad_in[h] += dot(low_turned, pre)
        grad_out[h] += dot(branch_turned, hidden[0, 0, h])
    scaled_one = one[0, 0].astype(F32)
    first = norm_back(back, scaled_one, inverse_one, gain_one)
    sums[0:1] += column_sum(back * scaled_one)
    sums[1:2] += column_sum(back)
    first_out[0, 0] = first
    mixed_out[0, 0] = first.astype(LOW)

    @pl.when(step == 2 * parts - 1)
    def _():
        half = grad_in.shape[1] // 2
        for total, (keep, give) in ((grad_in, halves[:2]), (grad_out, halves[2:])):
            low_half, high_half = total[:, :half].astype(LOW), total[:, half:].astype(LOW)
            keep[...] = jnp.where(core[0] == 0, low_half, high_half)
            give[...] = jnp.where(core[0] == 0, high_half, low_half)


def backward(plan, core, cotangents, low, one, two, scales, hidden, slope, vectors, weights):
    parts = plan.parts
    _, _, per, width = low.shape
    hid = hidden.shape[-1]
    tile = pl.BlockSpec((1, 1, per, width), lambda c, r: (c, r, 0, 0))
    wide = pl.BlockSpec((1, 1, parts, per, hid), lambda c, r: (c, r, 0, 0, 0))
    rows = (2, parts, per, width)
    return pl.pallas_call(
        functools.partial(backward_kernel, plan),
        grid=(2, parts),
        in_specs=[SCALARS]
        + [pl.BlockSpec((1, per, width), lambda c, r: (c, 0, 0))] * parts
        + [tile, tile, tile, pl.BlockSpec((1, 1, per, 128), lambda c, r: (c, r, 0, 0)), wide, wide]
        + [once(vectors.shape)]
        + [once(w.shape) for w in weights],
        out_specs=[
            tile,
            tile,
            once((8, width)),
            once((parts, hid)),
        ]
        + [once((parts, width // 2, hid))] * 4,
        out_shape=[
            jax.ShapeDtypeStruct(rows, F32),
            jax.ShapeDtypeStruct(rows, LOW),
            jax.ShapeDtypeStruct((8, width), F32),
            jax.ShapeDtypeStruct((parts, hid), F32),
        ]
        + [jax.ShapeDtypeStruct((parts, width // 2, hid), LOW)] * 4,
        scratch_shapes=[
            pltpu.VMEM((parts, width, hid), F32),
            pltpu.VMEM((parts, width, hid), F32),
            pltpu.VMEM((per, width), LOW),
        ],
        compiler_params=params(),
        cost_estimate=LONG,
        name="feed_backward",
    )(core, *cotangents, low, one, two, scales, hidden, slope, vectors, *weights)


def mix_back_kernel(plan, where, *refs):
    group, parts = plan.group, plan.parts
    pairs, (wave, cos_rows, sin_rows, first), outs, turned = (
        refs[:group],
        refs[group : group + 4],
        refs[-1 - parts : -1],
        refs[-1],
    )
    c, r = pl.program_id(0), pl.program_id(1)

    @pl.when((c == 0) & (r == 0))
    def _():
        turn_waves(plan, where, pairs, wave, turned, min(256, pairs[0].shape[1]))

    _, many, per, width = first.shape
    total = first[0].reshape(many * per, width) + section(cos_rows, sin_rows, turned, c)
    total = total.astype(LOW)
    for k in range(parts):

        @pl.when(r == k // many)
        def _(k=k):
            outs[k][0] = total[k % many * per : (k % many + 1) * per]


def mix_back(plan, where, pairs, wave, tables, first, after=()):
    parts = plan.parts
    _, _, per, width = first.shape
    rows = per * parts
    many = 2
    return pl.pallas_call(
        functools.partial(mix_back_kernel, plan),
        grid=(2, parts // many),
        in_specs=[SCALARS]
        + [once(pairs[0].shape)] * plan.group
        + [
            once(wave.shape),
            pl.BlockSpec((1, many * per, rows), lambda c, r: (c, r, 0)),
            pl.BlockSpec((1, many * per, rows), lambda c, r: (c, r, 0)),
            pl.BlockSpec((1, many, per, width), lambda c, r: (c, r, 0, 0)),
        ]
        + [LATER] * len(after),
        out_specs=[pl.BlockSpec((1, per, width), lambda c, r: (c, 0, 0))] * parts,
        out_shape=[jax.ShapeDtypeStruct((2, per, width), LOW)] * parts,
        scratch_shapes=[pltpu.VMEM((2, 2 * rows, width), LOW)],
        compiler_params=params(),
        cost_estimate=LIGHT,
        name="mix_backward",
    )(where, *pairs, wave, *tables, first, *after)


def add_split_kernel(bits, *refs):
    for k in range(2):
        one, two, keep, give = refs[2 * k], refs[2 * k + 1], refs[4 + 2 * k], refs[5 + 2 * k]
        total = (one[...].astype(F32) + two[...].astype(F32)).astype(LOW)
        half = keep.shape[1]
        low_half, high_half = total[:, :half], total[:, half:]
        keep[...] = jnp.where(bits[k] == 0, low_half, high_half)
        give[...] = jnp.where(bits[k] == 0, high_half, low_half)


def add_split(bits, pairs, cost):
    chunks, rows, hid = pairs[0][0].shape
    block = pl.BlockSpec((1, rows, hid), lambda h: (h, 0, 0))
    half = pl.BlockSpec((1, rows // 2, hid), lambda h: (h, 0, 0))
    outs = pl.pallas_call(
        add_split_kernel,
        grid=(chunks,),
        in_specs=[SCALARS] + [block] * 4,
        out_specs=[half] * 4,
        out_shape=[jax.ShapeDtypeStruct((chunks, rows // 2, hid), LOW)] * 4,
        compiler_params=params(),
        cost_estimate=cost,
        name="add_split",
    )(bits, *pairs[0], *pairs[1])
    return [outs[:2], outs[2:]]


def add_kernel(*refs):
    for k in range(2):
        total = refs[2 * k][...].astype(F32) + refs[2 * k + 1][...].astype(F32)
        refs[4 + k][...] = total.astype(LOW)


def add_pairs(pairs, cost):
    shape = pairs[0][0].shape
    block = pl.BlockSpec(shape, lambda: (0, 0, 0))
    return pl.pallas_call(
        add_kernel,
        in_specs=[block] * 4,
        out_specs=[block] * 2,
        out_shape=[jax.ShapeDtypeStruct(shape, LOW)] * 2,
        compiler_params=params(),
        cost_estimate=cost,
        name="add_pairs",
    )(*pairs[0], *pairs[1])


def finish_kernel(plan, where, core, perm, *refs):
    blocks, (in_own, in_other, out_own, out_other) = refs[: plan.parts], refs[plan.parts : plan.parts + 4]
    out, grad_in, grad_out, rows = refs[plan.parts + 4 :]
    unsort_kernel(plan, where, perm, *blocks, out, rows)
    half = in_own.shape[0]
    low_first = core[0] == 0
    own, other = in_own[...].astype(F32), in_other[...].astype(F32)
    grad_in[:half] = jnp.where(low_first, own, other)
    grad_in[half:] = jnp.where(low_first, other, own)
    own, other = out_own[...].astype(F32).T, out_other[...].astype(F32).T
    grad_out[:, :half] = jnp.where(low_first, own, other)
    grad_out[:, half:] = jnp.where(low_first, other, own)


def finish(plan, where, core, blocks, grads):
    _, per_rows, width = blocks[0].shape
    rows = per_rows * plan.parts
    size = min(SORTED, rows)
    per = size // plan.parts
    perm = unsorter(plan, size)
    half, hid = grads[0].shape
    step = math.gcd(hid, 256)
    last = hid // step - 1
    piece = pl.BlockSpec((half, step), lambda b: (0, jnp.minimum(b, last)))
    return pl.pallas_call(
        functools.partial(finish_kernel, plan),
        grid=(max(rows // size, last + 1),),
        in_specs=[SCALARS, SCALARS, whole((size, size))]
        + [pl.BlockSpec((2, per, width), lambda b: (0, jnp.minimum(b, rows // size - 1), 0))] * plan.parts
        + [piece] * 4,
        out_specs=[
            pl.BlockSpec((plan.seqs, size, width), lambda b: (0, jnp.minimum(b, rows // size - 1), 0)),
            pl.BlockSpec((2 * half, step), lambda b: (0, jnp.minimum(b, last))),
            pl.BlockSpec((step, 2 * half), lambda b: (jnp.minimum(b, last), 0)),
        ],
        out_shape=[
            jax.ShapeDtypeStruct((plan.seqs, rows, width), F32),
            jax.ShapeDtypeStruct((2 * half, hid), F32),
            jax.ShapeDtypeStruct((hid, 2 * half), F32),
        ],
        scratch_shapes=[pltpu.VMEM((size, width), LOW)],
        compiler_params=params(),
        cost_estimate=LIGHT,
        name="finish",
    )(where, core, perm, *blocks, *grads)


def angle_pair(steps, modulus):
    angle = (2.0 * math.pi / modulus) * (steps % modulus).astype(F32)
    return jnp.cos(angle), jnp.sin(angle)


def product_tables(coarse, fine, modulus, shape):
    cos_a, sin_a = angle_pair(coarse, modulus)
    cos_b, sin_b = angle_pair(fine, modulus)
    cos = (cos_a * cos_b - sin_a * sin_b).astype(LOW)
    sin = (sin_a * cos_b + cos_a * sin_b).astype(LOW)
    return cos.reshape(shape), sin.reshape(shape)


def width_table(index):
    width = index.shape[0]
    coarse = jnp.arange(width // 32, dtype=jnp.int32) * 32
    fine = jnp.arange(32, dtype=jnp.int32)
    pair = product_tables(
        (coarse[:, None] * index)[:, None, :], (fine[:, None] * index)[None], width, (width, width)
    )
    return jnp.concatenate(pair, axis=1)


def section_table(plan, g, b, rows):
    parts, group = plan.parts, plan.group
    length, per = rows * parts, rows // parts
    classes = jnp.asarray(plan.pairs, jnp.int32)
    steps = jnp.arange(per, dtype=jnp.int32)
    mine = lax.dynamic_index_in_dim(classes, g, 0, keepdims=False)
    cols = jnp.concatenate(
        [
            (lax.dynamic_index_in_dim(classes, g ^ j, 0, keepdims=False)[:, None] + parts * steps).reshape(-1)
            for j in range(group)
        ]
    )
    fine = jnp.arange(32, dtype=jnp.int32)
    coarse = jnp.concatenate([per * (b ^ r) + 32 * jnp.arange(per // 32, dtype=jnp.int32) for r in range(parts)])
    first = ((parts * coarse + mine[:, None])[:, :, None] * cols)[:, :, None, :]
    second = (parts * fine[:, None] * cols)[None, None]
    return product_tables(first, second, length, (2, rows, rows))


def body(plan, tokens, w_in, b_in, w_out, b_out, gain_one, shift_one, gain_two, shift_two, out_grad):
    seqs, rows, width = tokens.shape
    parts, group = plan.parts, plan.group
    hid = w_in.shape[1]
    d = lax.axis_index("dp")
    t = lax.axis_index("tensor")
    g = (t % plan.span) * 2 + d % 2
    b = (t // plan.span) % seqs * group + g
    where = jnp.stack([t, b, g]).astype(jnp.int32)

    def permute(value, perm):
        return lax.ppermute(value, BOTH, perm)

    def tie(values, *after):
        return lax.optimization_barrier((*values, *after))[: len(values)]

    z_bits = [1 << k for k in range(parts.bit_length() - 1)]
    slab_in, slab_out = width // plan.dp, hid // plan.dp
    flat_in = slab_in * hid // width
    packed = jnp.concatenate(
        [
            lax.dynamic_slice_in_dim(w_in, d * slab_in, slab_in, 0).reshape(flat_in, width),
            lax.dynamic_slice_in_dim(w_out, d * slab_out, slab_out, 0),
            jnp.pad(b_in[None], ((0, 15), (0, width - hid))),
        ]
    )
    sorted_tokens = sort_rows(plan, where, tokens)
    slabs = packed[None]
    for bit in reversed(z_bits):
        slabs = jnp.concatenate([slabs, permute(slabs, plan.xor_perm(0, bit))])
        if bit == z_bits[-1]:
            slabs, *sorted_tokens = tie([slabs, *sorted_tokens])
    taken_blocks = [permute(block, plan.out_perm(r)) for r, block in enumerate(sorted_tokens)]

    bias_in = slabs[:, flat_in + slab_out, :hid].astype(F32)
    slabs_in = slabs[:, :flat_in].reshape(parts, slab_in, hid)
    slabs_out = slabs[:, flat_in : flat_in + slab_out]
    if slabs_in.shape == slabs_out.shape:
        slabs_in = [jnp.concatenate([slabs_in, slabs_out])]
    else:
        slabs_in = [slabs_in, slabs_out]
    weights = [lax.all_gather(value, "dp", axis=1, tiled=True) for value in slabs_in]

    vectors = jnp.stack([b_out, gain_one, shift_one, gain_two, shift_two])
    late_g, late_b, index = tie([g, b, jnp.arange(width, dtype=jnp.int32)], taken_blocks[0])
    wave = width_table(index)
    tables = section_table(plan, late_g, late_b, rows)

    def send_back(blocks):
        return [permute(block, plan.back_perm(r)) for r, block in enumerate(blocks)]

    def exchange(folded):
        return [folded[0]] + [permute(folded[j], plan.group_perm(j)) for j in range(1, group)]

    sorted_grad = sort_rows(plan, where, out_grad, taken_blocks[:1])
    *folded, taken = fold(
        plan, where, taken_blocks, (wave, *tables, bias_in, vectors, sorted_grad[0]), LONG
    )
    sorted_grad = tie(sorted_grad, *taken_blocks)
    cotangents = [permute(block, plan.out_perm(r)) for r, block in enumerate(sorted_grad)]

    outs = forward(plan, where, exchange(folded), wave, tables, taken, bias_in, vectors, weights)
    acts, saved = send_back(outs[:parts]), outs[parts:]

    first, grad_mixed, sums, bias, *halves = backward(
        plan, (d % 2).astype(jnp.int32)[None], cotangents, *saved, vectors, weights
    )

    bits = [1 << k for k in range(plan.dp.bit_length() - 1)]
    orders = (bits, bits[:1] + bits[:0:-1])

    def bits_of(step):
        return jnp.stack([(d // order[step]) % 2 for order in orders]).astype(jnp.int32)

    def swap(pairs, step):
        return [
            (keep, permute(give, plan.xor_perm(order[step], 0)))
            for (keep, give), order in zip(pairs, orders)
        ]

    def tie_pairs(pairs, *after):
        flat = tie([x for pair in pairs for x in pair], *after)
        return [flat[:2], flat[2:]]

    halves = tie(halves, *acts)
    halves = add_split(bits_of(1), swap([halves[:2], halves[2:]], 0), LIGHT)

    folded = fold(plan, where, grad_mixed, acts)
    flat = [x for pair in halves for x in pair]
    grad_blocks = list(mix_back(plan, where, exchange(folded), wave, tables, first, flat))

    late = len(z_bits)
    returned = []

    def give_back(r, *after):
        block = tie([grad_blocks[r]], *after)[0] if after else grad_blocks[r]
        returned.append(permute(block, plan.back_perm(r)))

    for r in range(parts - late):
        give_back(r)
    small = jnp.concatenate([sums[:5], bias.reshape(-1, width)])
    small = tie([small], grad_blocks[0])[0]
    for k in range(1, len(bits)):
        pairs = tie_pairs(swap(halves, k), grad_blocks[0])
        if k + 1 < len(bits):
            halves = add_split(bits_of(k + 1), pairs, LONG)
    acts = tie(acts, *halves[0])
    activations = unsort_rows(plan, where, acts)
    totals = add_pairs(tie_pairs(pairs, activations, *returned), LIGHT)

    for bit in bits:
        small = small + permute(small, plan.xor_perm(bit, 0))
    small, bias = small[:5], small[5:].reshape(parts, hid)
    for step, bit in enumerate(z_bits):
        half = bias.shape[0] // 2
        pad = jnp.concatenate([small.reshape(-1), bias[half:].reshape(-1)])
        pad = tie([pad], totals[0])[0]
        got = permute(pad, plan.xor_perm(0, bit))
        chunks = [(value[: len(value) // 2], value[len(value) // 2 :]) for value in totals]
        pairs = [(keep, permute(give, plan.xor_perm(0, bit))) for keep, give in chunks]
        done = returned[-1:] if step else []
        give_back(len(returned), got)
        totals = add_pairs(tie_pairs(pairs, got, *done), LIGHT)
        small = small + got[: small.size].reshape(small.shape)
        bias = bias[:half] + got[small.size :].reshape(-1, hid)

    grads = []
    for value, order in zip(totals, orders):
        value = value[0]
        for bit in reversed(order[1:]):
            mine = (d // bit) % 2
            other = permute(value, plan.xor_perm(bit, 0))
            value = jnp.where(mine == 0, jnp.concatenate([value, other]), jnp.concatenate([other, value]))
        value = tie([value], returned[-1])[0]
        grads += [value, permute(value, plan.xor_perm(order[0], 0))]
    input_grad, grad_w_in, grad_w_out = finish(plan, where, (d % 2).astype(jnp.int32)[None], returned, grads)

    return (
        activations,
        input_grad,
        grad_w_in,
        bias[0],
        grad_w_out,
        small[4],
        small[0],
        small[1],
        small[2],
        small[3],
    )


def solution(mesh):
    def shards(tokens, *rest):
        return body(Plan(mesh, tokens.shape[0]), tokens, *rest)

    rows = P("dp", "tensor", None)
    return jax.shard_map(
        shards,
        mesh=mesh,
        in_specs=(rows, P(None, "tensor"), P("tensor"), P("tensor", None), P(), P(), P(), P(), P(), rows),
        out_specs=(rows, rows, P(None, "tensor"), P("tensor"), P("tensor", None), P(), P(), P(), P(), P()),
        check_vma=False,
    )
```

```python
import functools
import math

import jax
import jax.numpy as jnp
import numpy as np
from jax import lax
from jax.experimental import pallas as pl
from jax.experimental.pallas import tpu as pltpu
from jax.sharding import PartitionSpec as P

epsilon = 1e-12
LOW = jnp.bfloat16
F32 = jnp.float32
BOTH = ("dp", "tensor")
SORTED = 256
VMEM_BYTES = 60 * 1024 * 1024
LONG = pl.CostEstimate(flops=3 * 10**11, bytes_accessed=1 << 20, transcendentals=0)
LIGHT = pl.CostEstimate(flops=1024, bytes_accessed=1024, transcendentals=0)
GELU_C = math.sqrt(2.0 / math.pi)
GELU_A = 0.044715


def dot(left, right):
    return lax.dot_general(left, right, (((1,), (0,)), ((), ())), preferred_element_type=F32)


def dot_nt(left, right):
    return lax.dot_general(left, right, (((1,), (1,)), ((), ())), preferred_element_type=F32)


class Plan:
    def __init__(self, mesh, seqs):
        self.dp = mesh.shape["dp"]
        self.parts = mesh.shape["tensor"]
        self.seqs = seqs
        self.group = self.parts // seqs
        self.span = self.group // 2
        assert seqs == 2 and self.group >= 2 and self.parts & (self.parts - 1) == 0
        assert self.dp & (self.dp - 1) == 0
        self.pairs = [(0, self.group)] + [(g, self.parts - g) for g in range(1, self.group)]

    def flat(self, d, t):
        return d * self.parts + t

    def owner(self, core, block):
        seq, g = divmod(block, self.group)
        return g % 2, (core * self.seqs + seq) * self.span + g // 2

    def out_perm(self, r):
        perm = []
        for d in range(self.dp):
            for t in range(self.parts):
                core, chip = self.owner(d % 2, t ^ r)
                perm.append((self.flat(d, t), self.flat(d - d % 2 + core, chip)))
        return perm

    def back_perm(self, r):
        return [(dst, src) for src, dst in self.out_perm(r)]

    def group_perm(self, j):
        perm = []
        for d in range(self.dp):
            for t in range(self.parts):
                g = ((t % self.span) * 2 + d % 2) ^ j
                other = self.flat(d - d % 2 + g % 2, t - t % self.span + g // 2)
                perm.append((self.flat(d, t), other))
        return perm

    def xor_perm(self, dp_bits, z_bits):
        return [
            (self.flat(d, t), self.flat(d ^ dp_bits, t ^ z_bits))
            for d in range(self.dp)
            for t in range(self.parts)
        ]

    def fold_table(self):
        table = np.zeros((self.group, 2, self.parts), np.float32)
        for g in range(self.group):
            for q in range(self.parts):
                if g == 0:
                    table[g, :, q] = (1.0, (-1.0) ** q)
                else:
                    angle = 2.0 * math.pi * (q * g % self.parts) / self.parts
                    pair = (math.cos(angle), -math.sin(angle))
                    table[g, :, q] = [0.0 if abs(v) < 1e-9 else v for v in pair]
        return table


def whole(shape):
    return pl.BlockSpec(shape, lambda *_: (0,) * len(shape))


def once(shape):
    return pl.BlockSpec(shape, lambda *_: (0,) * len(shape), pipeline_mode=pl.Buffered(1))


SCALARS = pl.BlockSpec(memory_space=pltpu.SMEM)
LATER = pl.BlockSpec(memory_space=pl.ANY)


def params():
    return pltpu.CompilerParams(vmem_limit_bytes=VMEM_BYTES)


def block_order(plan, size):
    per = size // plan.parts
    return np.array([plan.parts * i + ka for pair in plan.pairs for ka in pair for i in range(per)])


def sort_kernel(plan, where, perm, value, *refs):
    outs = refs[-plan.parts :]
    per = perm.shape[0] // plan.parts
    for s in range(plan.seqs):
        rows = dot(perm[...], value[s].astype(LOW)).astype(LOW)
        for g in range(plan.group):
            piece = rows[g * 2 * per : (g + 1) * 2 * per].reshape(2, per, rows.shape[-1])
            r = (s * plan.group + g) ^ where[0]
            for k, out in enumerate(outs):

                @pl.when(r == k)
                def _(out=out, piece=piece):
                    out[...] = piece


def sort_rows(plan, where, value, after=()):
    seqs, rows, width = value.shape
    size = min(SORTED, rows)
    per = size // plan.parts
    order = block_order(plan, size)
    perm = jnp.asarray(order[:, None] == np.arange(size)[None, :], LOW)
    shape = jax.ShapeDtypeStruct((2, rows // plan.parts, width), LOW)
    return pl.pallas_call(
        functools.partial(sort_kernel, plan),
        grid=(rows // size,),
        in_specs=[SCALARS, whole((size, size)), pl.BlockSpec((seqs, size, width), lambda b: (0, b, 0))]
        + [LATER] * len(after),
        out_specs=[pl.BlockSpec((2, per, width), lambda b: (0, b, 0))] * plan.parts,
        out_shape=[shape] * plan.parts,
        compiler_params=params(),
        cost_estimate=LIGHT,
        name="sort_rows",
    )(where, perm, value, *after)


def unsorter(plan, size):
    return jnp.asarray(np.arange(size)[:, None] == block_order(plan, size)[None, :], LOW)


def unsort_kernel(plan, where, perm, *refs):
    blocks, out, rows = refs[: plan.parts], refs[-2], refs[-1]
    per = perm.shape[0] // plan.parts
    for s in range(plan.seqs):
        for g in range(plan.group):
            r = (s * plan.group + g) ^ where[0]
            for k, block in enumerate(blocks):

                @pl.when(r == k)
                def _(block=block, g=g):
                    rows[g * 2 * per : (g + 1) * 2 * per] = block[...].reshape(2 * per, rows.shape[-1])

        out[s] = dot(perm[...], rows[...])


def unsort_rows(plan, where, blocks):
    _, per_rows, width = blocks[0].shape
    rows = per_rows * plan.parts
    size = min(SORTED, rows)
    per = size // plan.parts
    perm = unsorter(plan, size)
    return pl.pallas_call(
        functools.partial(unsort_kernel, plan),
        grid=(rows // size,),
        in_specs=[SCALARS, whole((size, size))]
        + [pl.BlockSpec((2, per, width), lambda b: (0, b, 0))] * plan.parts,
        out_specs=pl.BlockSpec((plan.seqs, size, width), lambda b: (0, b, 0)),
        out_shape=jax.ShapeDtypeStruct((plan.seqs, rows, width), F32),
        scratch_shapes=[pltpu.VMEM((size, width), LOW)],
        compiler_params=params(),
        cost_estimate=LIGHT,
        name="unsort_rows",
    )(where, perm, *blocks)


def unsort_half_kernel(plan, half, where, perm, *refs):
    blocks, out, rows = refs[: plan.group], refs[-2], refs[-1]
    per = perm.shape[0] // plan.parts
    for g in range(plan.group):
        for k, block in enumerate(blocks):

            @pl.when((g ^ where[0]) % plan.group == k)
            def _(block=block, g=g):
                rows[g * 2 * per : (g + 1) * 2 * per] = block[...].reshape(2 * per, rows.shape[-1])

    out[0] = dot(perm[...], rows[...])


def unsort_half(plan, where, blocks, half, into=None):
    _, per_rows, width = blocks[0].shape
    rows = per_rows * plan.parts
    size = min(SORTED, rows)
    per = size // plan.parts
    perm = unsorter(plan, size)
    kept = [] if into is None else [into]
    return pl.pallas_call(
        functools.partial(unsort_half_kernel, plan, half),
        grid_spec=pltpu.PrefetchScalarGridSpec(
            num_scalar_prefetch=1,
            grid=(rows // size,),
            in_specs=[pl.BlockSpec((size, size), lambda b, where: (0, 0))]
            + [pl.BlockSpec((2, per, width), lambda b, where: (0, b, 0))] * plan.group
            + [LATER] * len(kept),
            out_specs=pl.BlockSpec(
                (1, size, width), lambda b, where: (where[0] // plan.group ^ half, b, 0)
            ),
            scratch_shapes=[pltpu.VMEM((size, width), LOW)],
        ),
        out_shape=jax.ShapeDtypeStruct((plan.seqs, rows, width), F32),
        input_output_aliases={2 + plan.group: 0} if kept else {},
        compiler_params=params(),
        cost_estimate=LIGHT,
        name="unsort_half",
    )(where, perm, *blocks, *kept)


def fold_kernel(plan, where, factors, *refs):
    parts, group = plan.parts, plan.group
    terms = [ref[0].astype(F32) for ref in refs[:parts]]
    outs, kept = refs[-1 - group : -1], refs[-1]
    for r in range(parts):
        kept[0, r] = refs[r][0]
    for j in range(group):
        for which in range(2):
            total = None
            for r in range(parts):
                place = ((where[2] ^ j) * 2 + which) * parts + (where[1] ^ r)
                term = factors[place] * terms[r]
                total = term if total is None else total + term
            outs[j][which] = total.astype(LOW)


def fold(plan, where, blocks, after=(), cost=LIGHT):
    parts = plan.parts
    _, per, width = blocks[0].shape
    step = min(256, per)
    steps = per // step
    stack = pl.BlockSpec((1, parts, step, width), lambda c, k: (c, 0, k, 0))
    single = pl.BlockSpec((1, step, width), lambda c, k: (c, k, 0))
    out = pl.BlockSpec((2, step, width), lambda c, k: (0, c * steps + k, 0))
    return pl.pallas_call(
        functools.partial(fold_kernel, plan),
        grid=(2, steps),
        in_specs=[SCALARS, SCALARS] + [single] * parts + [LATER] * len(after),
        out_specs=[out] * plan.group + [stack],
        out_shape=[jax.ShapeDtypeStruct((2, 2 * per, width), LOW)] * plan.group
        + [jax.ShapeDtypeStruct((2, parts, per, width), LOW)],
        compiler_params=params(),
        cost_estimate=cost,
        name="fold_parts",
    )(where, jnp.asarray(plan.fold_table().reshape(-1)), *blocks, *after)


def turn_waves(plan, where, pairs, wave, turned, step):
    first = jnp.where(where[2] == 0, 1.0, 0.0).astype(F32)
    rest = 1.0 - first
    width = wave.shape[0]
    own = pairs[0].shape[1]
    rows = own * plan.group
    for j, pair in enumerate(pairs):
        for k in range(own // step):
            span = slice(k * step, (k + 1) * step)
            pw = dot(pair[0, span], wave[...])
            qw = dot(pair[1, span], wave[...])
            pc, ps, qc, qs = pw[:, :width], pw[:, width:], qw[:, :width], qw[:, width:]
            at = j * own + k * step
            turned[0, at : at + step] = (pc + rest * qs).astype(LOW)
            turned[0, rows + at : rows + at + step] = (rest * qc - ps).astype(LOW)
            turned[1, at : at + step] = (first * qc + rest * (pc - qs)).astype(LOW)
            turned[1, rows + at : rows + at + step] = (-first * qs - rest * (qc + ps)).astype(LOW)


def normed(resid, gain, shift):
    centered = resid - jnp.mean(resid, axis=-1, keepdims=True)
    inverse = lax.rsqrt(jnp.mean(centered * centered, axis=-1, keepdims=True) + epsilon)
    scaled = centered * inverse
    return scaled * gain + shift, scaled, inverse


def forward_kernel(plan, where, *refs):
    group, parts = plan.group, plan.parts
    pairs, refs = refs[:group], refs[group:]
    (wave, cos_rows, sin_rows, taken, b_in, vectors, *refs) = refs
    (w_in, w_out), refs, copies = split_weights(plan, where, refs)
    acts, (low_out, one_out, two_out, scales, hidden_out, slope_out, turned) = refs[:parts], refs[parts:]
    c, r = pl.program_id(0), pl.program_id(1)
    _, many, per, width = taken.shape
    rows = many * per

    @pl.when((c == 0) & (r == 0))
    def _():
        for copy in copies():
            copy.start()
        turn_waves(plan, where, pairs, wave, turned, min(256, pairs[0].shape[1]))
        for copy in copies():
            copy.wait()

    mixed = section(cos_rows, sin_rows, turned, c)
    b_out, gain_one, shift_one, gain_two, shift_two = (vectors[k : k + 1] for k in range(5))
    resid = taken[0].reshape(rows, width).astype(F32) + mixed
    normed_one, scaled_one, inverse_one = normed(resid, gain_one, shift_one)
    low = normed_one.astype(LOW)
    low_out[0] = low.reshape(many, per, width)
    one_out[0] = scaled_one.astype(LOW).reshape(many, per, width)
    branch = normed_one + b_out
    for h in range(parts):
        pre = dot(low, w_in[h]) + b_in[h : h + 1]
        square = pre * pre
        bend = jnp.tanh(pre * (GELU_C + (GELU_C * GELU_A) * square))
        half = 0.5 * pre
        hidden = (half + half * bend).astype(LOW)
        slope = 0.5 + 0.5 * bend + half * (1.0 - bend * bend) * (GELU_C + (3.0 * GELU_C * GELU_A) * square)
        hidden_out[0, :, h] = hidden.reshape(many, per, hidden.shape[1])
        slope_out[0, :, h] = slope.astype(LOW).reshape(many, per, hidden.shape[1])
        branch = branch + dot(hidden, w_out[h])
    normed_two, scaled_two, inverse_two = normed(branch, gain_two, shift_two)
    two_out[0] = scaled_two.astype(LOW).reshape(many, per, width)
    lanes = lax.broadcasted_iota(jnp.int32, (rows, 128), 1)
    scales[0] = jnp.where(lanes == 0, inverse_one, inverse_two).reshape(many, per, 128)
    act = normed_two.astype(LOW)
    for k in range(parts):

        @pl.when(r == k // many)
        def _(k=k):
            acts[k][0] = act[k % many * per : (k % many + 1) * per]


def section(cos_rows, sin_rows, turned, c):
    rows = cos_rows.shape[2]
    return dot(cos_rows[0], turned[c, :rows]) + dot(sin_rows[0], turned[c, rows:])


def weight_specs(plan, weights):
    return [LATER if plan.slabs else once(w.shape) for w in weights]


def weight_scratch(plan, weights):
    if not plan.slabs:
        return []
    chunks, slab, hid = weights[0].shape
    return [
        pltpu.VMEM((chunks, slab * len(weights), hid), LOW),
        pltpu.SemaphoreType.DMA((len(weights),)),
    ]


def slab_copies(plan, where, slabs, room, sems):
    slab = slabs[0].shape[1]
    for j, ref in enumerate(slabs):
        at = pl.multiple_of((where[4] ^ j) * slab, 16)
        yield pltpu.make_async_copy(ref, room.at[:, pl.ds(at, slab)], sems.at[j])


def split_weights(plan, where, refs):
    if plan.slabs:
        slabs, refs, room, sems = refs[: plan.dp], refs[plan.dp : -2], refs[-2], refs[-1]

        def copies():
            return slab_copies(plan, where, slabs, room, sems)

        return (room.at[: plan.parts], room.at[plan.parts :]), refs, copies
    return refs[:2], refs[2:], lambda: ()


def forward(plan, where, pairs, wave, tables, taken, b_in, vectors, weights):
    parts = plan.parts
    _, _, per, width = taken.shape
    rows = per * parts
    hid = b_in.shape[1]
    many = 1
    tile = pl.BlockSpec((1, many, per, width), lambda c, r: (c, r, 0, 0))
    wide = pl.BlockSpec((1, many, parts, per, hid), lambda c, r: (c, r, 0, 0, 0))
    low = jax.ShapeDtypeStruct((2, parts, per, width), LOW)
    big = jax.ShapeDtypeStruct((2, parts, parts, per, hid), LOW)
    return pl.pallas_call(
        functools.partial(forward_kernel, plan),
        grid=(2, parts // many),
        in_specs=[SCALARS]
        + [once(pairs[0].shape)] * plan.group
        + [
            once(wave.shape),
            pl.BlockSpec((1, many * per, rows), lambda c, r: (c, r, 0)),
            pl.BlockSpec((1, many * per, rows), lambda c, r: (c, r, 0)),
            tile,
            once(b_in.shape),
            once(vectors.shape),
        ]
        + weight_specs(plan, weights),
        out_specs=[pl.BlockSpec((1, per, width), lambda c, r: (c, 0, 0))] * parts
        + [tile, tile, tile, pl.BlockSpec((1, many, per, 128), lambda c, r: (c, r, 0, 0)), wide, wide],
        out_shape=[jax.ShapeDtypeStruct((2, per, width), LOW)] * parts
        + [low, low, low, jax.ShapeDtypeStruct((2, parts, per, 128), F32), big, big],
        scratch_shapes=[pltpu.VMEM((2, 2 * rows, width), LOW)] + weight_scratch(plan, weights),
        compiler_params=params(),
        cost_estimate=LIGHT,
        name="mix_forward",
    )(where, *pairs, wave, *tables, taken, b_in, vectors, *weights)


def norm_back(grad, scaled, inverse, gain):
    grad_scaled = grad * gain
    return inverse * (
        grad_scaled
        - jnp.mean(grad_scaled, axis=-1, keepdims=True)
        - scaled * jnp.mean(grad_scaled * scaled, axis=-1, keepdims=True)
    )


def column_sum(value):
    return jnp.sum(value, axis=0, keepdims=True)


def backward_kernel(plan, tiles, where, factors, *refs):
    parts, group = plan.parts, plan.group
    cotangents, refs = refs[:parts], refs[parts:]
    (two, scales_two, low, hidden, slope, one, scales_one, vectors, *refs) = refs
    (w_in, w_out), refs, copies = split_weights(plan, where, refs)
    (first_out, sums, bias, *refs) = refs
    folded, halves, refs = refs[:group], refs[group : group + 4], refs[group + 4 :]
    (grad_in, grad_out, cotangent, coming, coming_low, branch, total, leaving, rounded, *refs) = refs
    stages, sems = refs[:4], refs[4]
    step = pl.program_id(0)
    gain_one, gain_two = vectors[1:2], vectors[3:4]
    half = grad_in.shape[1] // 2

    def norm_two():
        r = lax.rem(step, parts)
        for k in range(parts):

            @pl.when(r == k)
            def _(k=k):
                cotangent[...] = cotangents[k][0]

    def stage_two():
        grad = cotangent[...].astype(F32)
        scaled = two[0, 0].astype(F32)
        second = norm_back(grad, scaled, scales_two[0, 0, :, 1:2], gain_two)
        second_low = second.astype(LOW)
        sums[2:3] += column_sum(grad * scaled)
        sums[3:4] += column_sum(grad)
        sums[4:5] += column_sum(second_low.astype(F32))
        coming[...] = second
        coming_low[...] = second_low

    def turn_over():
        leaving[...] = total[...]
        total[...] = coming[...]
        branch[...] = coming_low[...]

    def feed(last):
        low_turned = low[0, 0].T
        branch_turned = branch[...].T
        for h in range(parts):
            pre = (dot_nt(branch[...], w_out[h]) * slope[0, 0, h].astype(F32)).astype(LOW)
            bias[h : h + 1] += column_sum(pre.astype(F32))
            total[...] += dot_nt(pre, w_in[h])
            grads = (dot(low_turned, pre), dot(branch_turned, hidden[0, 0, h]))
            if not last:
                grad_in[h] += grads[0]
                grad_out[h] += grads[1]
                continue
            for k, (kept, grad) in enumerate(zip((grad_in, grad_out), grads)):
                grad = (kept[h] + grad).astype(LOW)
                stages[2 * k][h] = jnp.where(where[3] == 0, grad[:half], grad[half:])
                stages[2 * k + 1][h] = jnp.where(where[3] == 0, grad[half:], grad[:half])
            for k in range(4):
                pltpu.make_async_copy(stages[k].at[h], halves[k].at[h], sems.at[k, h]).start()

    def norm_one(valid):
        back = jnp.where(valid, leaving[...], 0.0)
        scaled = one[0, 0].astype(F32)
        first = norm_back(back, scaled, scales_one[0, 0, :, 0:1], gain_one)
        sums[0:1] += column_sum(back * scaled)
        sums[1:2] += column_sum(back)
        first_out[0, 0] = first
        rounded[lax.rem(jnp.maximum(step - 2, 0), parts)] = first.astype(LOW)

    def fold_all():
        for j in range(group):
            for which in range(2):
                value = None
                for r in range(parts):
                    place = ((where[2] ^ j) * 2 + which) * parts + (where[1] ^ r)
                    term = factors[place] * rounded[r].astype(F32)
                    value = term if value is None else value + term
                folded[j][which] = value.astype(LOW)

    @pl.when(step == 0)
    def _():
        for copy in copies():
            copy.start()
        sums[...] = jnp.zeros_like(sums)
        bias[...] = jnp.zeros_like(bias)
        grad_in[...] = jnp.zeros_like(grad_in)
        grad_out[...] = jnp.zeros_like(grad_out)

    @pl.when(step < tiles)
    def _():
        norm_two()

    @pl.when(step == 0)
    def _():
        stage_two()
        for copy in copies():
            copy.wait()

    @pl.when((step > 0) & (step < tiles))
    def _():
        turn_over()
        stage_two()
        feed(False)
        norm_one(step > 1)

    @pl.when(step == tiles)
    def _():
        turn_over()
        feed(True)
        norm_one(True)

    @pl.when(step == tiles + 1)
    def _():
        leaving[...] = total[...]
        norm_one(True)

    @pl.when((step > 1) & (lax.rem(step - 1, parts) == 0))
    def _():
        fold_all()

    @pl.when(step == tiles + 1)
    def _():
        for k in range(4):
            for h in range(parts):
                pltpu.make_async_copy(stages[k].at[h], halves[k].at[h], sems.at[k, h]).wait()


def backward(plan, where, cotangents, low, one, two, scales, hidden, slope, vectors, weights):
    parts, group = plan.parts, plan.group
    _, _, per, width = low.shape
    hid = hidden.shape[-1]
    tiles = 2 * parts

    def tile(lag, *rest):
        def place(s):
            at = jnp.clip(s - lag, 0, tiles - 1)
            return (at // parts, at % parts) + (0,) * len(rest)

        return pl.BlockSpec((1, 1, *rest), place)

    def class_of(lag):
        return lambda s: jnp.clip(s - lag, 0, tiles - 1) // parts

    half = jax.ShapeDtypeStruct((parts, width // 2, hid), LOW)
    return pl.pallas_call(
        functools.partial(backward_kernel, plan, tiles),
        grid=(tiles + 2,),
        in_specs=[SCALARS, SCALARS]
        + [pl.BlockSpec((1, per, width), lambda s: (class_of(0)(s), 0, 0))] * parts
        + [
            tile(0, per, width),
            tile(0, per, 128),
            tile(1, per, width),
            tile(1, parts, per, hid),
            tile(1, parts, per, hid),
            tile(2, per, width),
            tile(2, per, 128),
            once(vectors.shape),
        ]
        + weight_specs(plan, weights),
        out_specs=[tile(2, per, width), once((8, width)), once((parts, hid))]
        + [pl.BlockSpec((2, per, width), lambda s: (0, class_of(2)(s), 0))] * group
        + [LATER] * 4,
        out_shape=[
            jax.ShapeDtypeStruct((2, parts, per, width), F32),
            jax.ShapeDtypeStruct((8, width), F32),
            jax.ShapeDtypeStruct((parts, hid), F32),
        ]
        + [jax.ShapeDtypeStruct((2, 2 * per, width), LOW)] * group
        + [half] * 4,
        scratch_shapes=[
            pltpu.VMEM((parts, width, hid), F32),
            pltpu.VMEM((parts, width, hid), F32),
            pltpu.VMEM((per, width), LOW),
            pltpu.VMEM((per, width), F32),
            pltpu.VMEM((per, width), LOW),
            pltpu.VMEM((per, width), LOW),
            pltpu.VMEM((per, width), F32),
            pltpu.VMEM((per, width), F32),
            pltpu.VMEM((parts, per, width), LOW),
        ]
        + [pltpu.VMEM(half.shape, LOW)] * 4
        + [pltpu.SemaphoreType.DMA((4, parts))]
        + weight_scratch(plan, weights),
        compiler_params=params(),
        cost_estimate=LONG,
        name="feed_backward",
    )(
        where,
        jnp.asarray(plan.fold_table().reshape(-1)),
        *cotangents,
        two,
        scales,
        low,
        hidden,
        slope,
        one,
        scales,
        vectors,
        *weights,
    )


def mix_back_kernel(plan, where, *refs):
    group = plan.group
    pairs, (wave, cos_rows, sin_rows, first), outs, turned = (
        refs[:group],
        refs[group : group + 4],
        refs[-1 - group : -1],
        refs[-1],
    )
    c, r = pl.program_id(0), pl.program_id(1)
    _, many, per, width = first.shape

    @pl.when((c == 0) & (r == 0))
    def _():
        turn_waves(plan, where, pairs, wave, turned, min(256, pairs[0].shape[1]))

    total = first[0].reshape(many * per, width) + section(cos_rows, sin_rows, turned, c)
    total = total.astype(LOW)
    for k in range(group):

        @pl.when(r == k // many)
        def _(k=k):
            outs[k][0] = total[k % many * per : (k % many + 1) * per]


def mix_back(plan, where, pairs, wave, tables, first, half, after=(), cost=LIGHT):
    parts, group = plan.parts, plan.group
    _, _, per, width = first.shape
    rows = per * parts
    many = 2
    begin = half * group // many
    return pl.pallas_call(
        functools.partial(mix_back_kernel, plan),
        grid=(2, group // many),
        in_specs=[SCALARS]
        + [once(pairs[0].shape)] * group
        + [
            once(wave.shape),
            pl.BlockSpec((1, many * per, rows), lambda c, r: (c, begin + r, 0)),
            pl.BlockSpec((1, many * per, rows), lambda c, r: (c, begin + r, 0)),
            pl.BlockSpec((1, many, per, width), lambda c, r: (c, begin + r, 0, 0)),
        ]
        + [LATER] * len(after),
        out_specs=[pl.BlockSpec((1, per, width), lambda c, r: (c, 0, 0))] * group,
        out_shape=[jax.ShapeDtypeStruct((2, per, width), LOW)] * group,
        scratch_shapes=[pltpu.VMEM((2, 2 * rows, width), LOW)],
        compiler_params=params(),
        cost_estimate=cost,
        name="mix_backward",
    )(where, *pairs, wave, *tables, first, *after)


def add_split_kernel(bits, *refs):
    for k in range(2):
        one, two, keep, give = refs[2 * k], refs[2 * k + 1], refs[4 + 2 * k], refs[5 + 2 * k]
        total = (one[...].astype(F32) + two[...].astype(F32)).astype(LOW)
        half = keep.shape[1]
        low_half, high_half = total[:, :half], total[:, half:]
        keep[...] = jnp.where(bits[k] == 0, low_half, high_half)
        give[...] = jnp.where(bits[k] == 0, high_half, low_half)


def add_split(bits, pairs, cost):
    chunks, rows, hid = pairs[0][0].shape
    block = pl.BlockSpec((1, rows, hid), lambda h: (h, 0, 0))
    half = pl.BlockSpec((1, rows // 2, hid), lambda h: (h, 0, 0))
    outs = pl.pallas_call(
        add_split_kernel,
        grid=(chunks,),
        in_specs=[SCALARS] + [block] * 4,
        out_specs=[half] * 4,
        out_shape=[jax.ShapeDtypeStruct((chunks, rows // 2, hid), LOW)] * 4,
        compiler_params=params(),
        cost_estimate=cost,
        name="add_split",
    )(bits, *pairs[0], *pairs[1])
    return [outs[:2], outs[2:]]


def add_spread_kernel(order, *refs):
    for k in range(2):
        total = (refs[2 * k][...].astype(F32) + refs[2 * k + 1][...].astype(F32)).astype(LOW)
        for at, chunk in enumerate(order):
            refs[4 + chunk][k] = total[at]


def add_spread(order, pairs):
    chunks, rows, hid = pairs[0][0].shape
    block = pl.BlockSpec((chunks, rows, hid), lambda: (0, 0, 0))
    return pl.pallas_call(
        functools.partial(add_spread_kernel, order),
        in_specs=[block] * 4,
        out_specs=[pl.BlockSpec((2, rows, hid), lambda: (0, 0, 0))] * chunks,
        out_shape=[jax.ShapeDtypeStruct((2, rows, hid), LOW)] * chunks,
        compiler_params=params(),
        cost_estimate=LIGHT,
        name="add_spread",
    )(*pairs[0], *pairs[1])


def add_all_kernel(*refs):
    total = refs[0][...].astype(F32)
    for ref in refs[1:-1]:
        total = total + ref[...].astype(F32)
    refs[-1][...] = total.astype(LOW)


def add_all(values):
    block = pl.BlockSpec(values[0].shape, lambda: (0, 0, 0))
    return pl.pallas_call(
        add_all_kernel,
        in_specs=[block] * len(values),
        out_specs=block,
        out_shape=jax.ShapeDtypeStruct(values[0].shape, LOW),
        compiler_params=params(),
        cost_estimate=LIGHT,
        name="add_all",
    )(*values)


def finish_kernel(places, *refs):
    blocks, (grad_in, grad_out, rows) = refs[:-3], refs[-3:]
    slab = blocks[0].shape[1]
    for j, block in enumerate(blocks):
        for k, out in enumerate((grad_in, rows)):
            at = pl.multiple_of(places[k * len(blocks) + j] * slab, 8)
            out[pl.ds(at, slab)] = block[k].astype(F32)
    grad_out[...] = rows[...].T


def finish(places, blocks):
    _, slab, hid = blocks[0].shape
    width = slab * len(blocks)
    step = math.gcd(hid, 256)
    return pl.pallas_call(
        finish_kernel,
        grid=(hid // step,),
        in_specs=[SCALARS] + [pl.BlockSpec((2, slab, step), lambda h: (0, 0, h))] * len(blocks),
        out_specs=[
            pl.BlockSpec((width, step), lambda h: (0, h)),
            pl.BlockSpec((step, width), lambda h: (h, 0)),
        ],
        out_shape=[
            jax.ShapeDtypeStruct((width, hid), F32),
            jax.ShapeDtypeStruct((hid, width), F32),
        ],
        scratch_shapes=[pltpu.VMEM((width, step), F32)],
        compiler_params=params(),
        cost_estimate=LIGHT,
        name="finish_weights",
    )(places, *blocks)


def angle_pair(steps, modulus):
    angle = (2.0 * math.pi / modulus) * (steps % modulus).astype(F32)
    return jnp.cos(angle), jnp.sin(angle)


def product_tables(coarse, fine, modulus, shape):
    cos_a, sin_a = angle_pair(coarse, modulus)
    cos_b, sin_b = angle_pair(fine, modulus)
    cos = (cos_a * cos_b - sin_a * sin_b).astype(LOW)
    sin = (sin_a * cos_b + cos_a * sin_b).astype(LOW)
    return cos.reshape(shape), sin.reshape(shape)


def width_table(index):
    width = index.shape[0]
    coarse = jnp.arange(width // 32, dtype=jnp.int32) * 32
    fine = jnp.arange(32, dtype=jnp.int32)
    pair = product_tables(
        (coarse[:, None] * index)[:, None, :], (fine[:, None] * index)[None], width, (width, width)
    )
    return jnp.concatenate(pair, axis=1)


def section_table(plan, g, b, rows):
    parts, group = plan.parts, plan.group
    length, per = rows * parts, rows // parts
    classes = jnp.asarray(plan.pairs, jnp.int32)
    steps = jnp.arange(per, dtype=jnp.int32)
    mine = lax.dynamic_index_in_dim(classes, g, 0, keepdims=False)
    cols = jnp.concatenate(
        [
            (lax.dynamic_index_in_dim(classes, g ^ j, 0, keepdims=False)[:, None] + parts * steps).reshape(-1)
            for j in range(group)
        ]
    )
    fine = jnp.arange(32, dtype=jnp.int32)
    coarse = jnp.concatenate([per * (b ^ r) + 32 * jnp.arange(per // 32, dtype=jnp.int32) for r in range(parts)])
    first = ((parts * coarse + mine[:, None])[:, :, None] * cols)[:, :, None, :]
    second = (parts * fine[:, None] * cols)[None, None]
    return product_tables(first, second, length, (2, rows, rows))


def body(plan, tokens, w_in, b_in, w_out, b_out, gain_one, shift_one, gain_two, shift_two, out_grad):
    seqs, rows, width = tokens.shape
    parts, group = plan.parts, plan.group
    hid = w_in.shape[1]
    d = lax.axis_index("dp")
    t = lax.axis_index("tensor")
    g = (t % plan.span) * 2 + d % 2
    b = (t // plan.span) % seqs * group + g
    where = jnp.stack([t, b, g, d % 2, d]).astype(jnp.int32)

    def permute(value, perm):
        return lax.ppermute(value, BOTH, perm)

    def tie(values, *after):
        return lax.optimization_barrier((*values, *after))[: len(values)]

    def over_pairs(own):
        blocks = {0: own}
        for j in range(2, plan.dp, 2):
            blocks[j] = permute(own, plan.xor_perm(j, 0))
        for j in range(0, plan.dp, 2):
            blocks[j + 1] = permute(blocks[j], plan.xor_perm(1, 0))
        return [blocks[j] for j in range(plan.dp)]

    z_bits = [1 << k for k in range(parts.bit_length() - 1)]
    slab_in, slab_out = width // plan.dp, hid // plan.dp
    flat_in = slab_in * hid // width
    packed = jnp.concatenate(
        [
            lax.dynamic_slice_in_dim(w_in, d * slab_in, slab_in, 0).reshape(flat_in, width),
            lax.dynamic_slice_in_dim(w_out, d * slab_out, slab_out, 0),
            jnp.pad(b_in[None], ((0, 15), (0, width - hid))),
        ]
    )
    sorted_tokens = sort_rows(plan, where, tokens)
    slabs, z_order = packed[None], [0]
    for bit in reversed(z_bits):
        z_order += [other ^ bit for other in z_order]
        slabs = jnp.concatenate([slabs, permute(slabs, plan.xor_perm(0, bit))])
        if bit == z_bits[-1]:
            slabs, *sorted_tokens = tie([slabs, *sorted_tokens])
    taken_blocks = [permute(block, plan.out_perm(r)) for r, block in enumerate(sorted_tokens)]

    bias_in = slabs[:, flat_in + slab_out, :hid].astype(F32)
    slabs_in = slabs[:, :flat_in].reshape(parts, slab_in, hid)
    slabs_out = slabs[:, flat_in : flat_in + slab_out]
    plan.slabs = slabs_in.shape == slabs_out.shape and slab_in % 16 == 0
    if plan.slabs:
        weights = over_pairs(tie([jnp.concatenate([slabs_in, slabs_out])], taken_blocks[0])[0])
    else:
        weights = [lax.all_gather(value, "dp", axis=1, tiled=True) for value in (slabs_in, slabs_out)]

    vectors = jnp.stack([b_out, gain_one, shift_one, gain_two, shift_two])
    late_g, late_b, index = tie([g, b, jnp.arange(width, dtype=jnp.int32)], taken_blocks[0])
    wave = width_table(index)
    tables = section_table(plan, late_g, late_b, rows)

    def send_back(blocks):
        return [permute(block, plan.back_perm(r)) for r, block in enumerate(blocks)]

    def exchange(folded):
        return [folded[0]] + [permute(folded[j], plan.group_perm(j)) for j in range(1, group)]

    sorted_grad = sort_rows(plan, where, out_grad, taken_blocks[:1])
    *folded, taken = fold(
        plan, where, taken_blocks, (wave, *tables, bias_in, vectors, sorted_grad[0]), LONG
    )
    sorted_grad = tie(sorted_grad, *taken_blocks)
    cotangents = [permute(block, plan.out_perm(r)) for r, block in enumerate(sorted_grad)]

    outs = forward(plan, where, exchange(folded), wave, tables, taken, bias_in, vectors, weights)
    acts, saved = send_back(outs[:parts]), outs[parts:]

    first, sums, bias, *rest = backward(plan, where, cotangents, *saved, vectors, weights)
    folded, halves = rest[:group], rest[group:]

    bits = [1 << k for k in range(plan.dp.bit_length() - 1)]
    orders = (bits, bits[:1] + bits[:0:-1])

    def bits_of(step):
        return jnp.stack([(d // order[step]) % 2 for order in orders]).astype(jnp.int32)

    def swap(pairs, step):
        return [
            (keep, permute(give, plan.xor_perm(order[step], 0)))
            for (keep, give), order in zip(pairs, orders)
        ]

    def tie_pairs(pairs, *after):
        flat = tie([x for pair in pairs for x in pair], *after)
        return [flat[:2], flat[2:]]

    def tree(values):
        while len(values) > 1:
            values = [one + two for one, two in zip(values[::2], values[1::2])]
        return values[0]

    folded = tie(folded, *acts)
    exchanged = exchange(folded)
    grad_blocks = list(mix_back(plan, where, exchanged, wave, tables, first, 0))
    halves = tie(halves, *exchanged)
    pairs = tie_pairs(swap([halves[:2], halves[2:]], 0), grad_blocks[0])
    halves = add_split(bits_of(1), pairs, LIGHT)
    flat = [x for pair in halves for x in pair]
    grad_blocks += mix_back(plan, where, exchanged, wave, tables, first, 1, flat, LONG)

    returned = []

    def give_back(r, *after):
        block = tie([grad_blocks[r]], *after)[0] if after else grad_blocks[r]
        returned.append(permute(block, plan.back_perm(r)))

    for r in range(group):
        give_back(r)
    activations = unsort_rows(plan, where, tie(acts, grad_blocks[-1]))
    for k in range(1, len(bits) - 1):
        halves = add_split(bits_of(k + 1), tie_pairs(swap(halves, k), activations), LIGHT)
    for r in range(group, parts - 1):
        give_back(r, *returned[:group], activations)
    pairs = tie_pairs(swap(halves, len(bits) - 1), activations, *returned)
    chunks = add_spread(z_order, pairs)

    values = [chunks[0]] + [permute(chunks[k], plan.xor_perm(0, k)) for k in range(1, parts)]
    input_grad = unsort_half(plan, where, returned[:group], 0)
    small = tie([jnp.concatenate([sums[:5], bias.reshape(-1, width)])], input_grad, chunks[0])[0]
    for bit in bits:
        small = small + permute(small, plan.xor_perm(bit, 0))
    flat_sums, bias = small[:5].reshape(-1), small[5:].reshape(parts, hid)
    pads = [jnp.concatenate([flat_sums, bias[z_order.index(k)]]) for k in range(parts)]
    got = [pads[0]] + [permute(pads[k], plan.xor_perm(0, k)) for k in range(1, parts)]
    small = tree(got)
    give_back(parts - 1, *values, small)
    total = add_all(values)
    blocks = {0: total}
    for j in range(2, plan.dp, 2):
        blocks[j] = permute(total, plan.xor_perm(j, 0))
    input_grad = unsort_half(plan, where, returned[group:], 1, input_grad)
    blocks[plan.dp - 2] = tie([blocks[plan.dp - 2]], input_grad)[0]
    for j in range(0, plan.dp, 2):
        blocks[j + 1] = permute(blocks[j], plan.xor_perm(1, 0))
    blocks = [blocks[j] for j in range(plan.dp)]
    places = [
        sum((((d ^ j) // bit) % 2) * (plan.dp >> k + 1) for k, bit in enumerate(order))
        for order in orders
        for j in range(plan.dp)
    ]
    grad_w_in, grad_w_out = finish(jnp.stack(places).astype(jnp.int32), blocks)
    return (
        activations,
        input_grad,
        grad_w_in,
        small[5 * width :],
        grad_w_out,
        *(small[k * width : (k + 1) * width] for k in (4, 0, 1, 2, 3)),
    )


def solution(mesh):
    def shards(tokens, *rest):
        return body(Plan(mesh, tokens.shape[0]), tokens, *rest)

    rows = P("dp", "tensor", None)
    return jax.shard_map(
        shards,
        mesh=mesh,
        in_specs=(rows, P(None, "tensor"), P("tensor"), P("tensor", None), P(), P(), P(), P(), P(), rows),
        out_specs=(rows, rows, P(None, "tensor"), P("tensor"), P("tensor", None), P(), P(), P(), P(), P()),
        check_vma=False,
    )
```

```python
import functools
import math

import jax
import jax.numpy as jnp
import numpy as np
from jax import lax
from jax.experimental import pallas as pl
from jax.experimental.pallas import tpu as pltpu
from jax.sharding import PartitionSpec as P

epsilon = 1e-12
LOW = jnp.bfloat16
F32 = jnp.float32
BOTH = ("dp", "tensor")
SORTED = 256
VMEM_BYTES = 60 * 1024 * 1024
LONG = pl.CostEstimate(flops=3 * 10**11, bytes_accessed=1 << 20, transcendentals=0)
LIGHT = pl.CostEstimate(flops=1024, bytes_accessed=1024, transcendentals=0)
GELU_C = math.sqrt(2.0 / math.pi)
GELU_A = 0.044715


def dot(left, right):
    return lax.dot_general(left, right, (((1,), (0,)), ((), ())), preferred_element_type=F32)


def dot_nt(left, right):
    return lax.dot_general(left, right, (((1,), (1,)), ((), ())), preferred_element_type=F32)


class Plan:
    def __init__(self, mesh, seqs):
        self.dp = mesh.shape["dp"]
        self.parts = mesh.shape["tensor"]
        self.seqs = seqs
        self.group = self.parts // seqs
        self.span = self.group // 2
        assert seqs == 2 and self.group >= 2 and self.parts & (self.parts - 1) == 0
        assert self.dp & (self.dp - 1) == 0
        self.pairs = [(0, self.group)] + [(g, self.parts - g) for g in range(1, self.group)]

    def flat(self, d, t):
        return d * self.parts + t

    def owner(self, core, block):
        seq, g = divmod(block, self.group)
        return g % 2, (core * self.seqs + seq) * self.span + g // 2

    def out_perm(self, r):
        perm = []
        for d in range(self.dp):
            for t in range(self.parts):
                core, chip = self.owner(d % 2, t ^ r)
                perm.append((self.flat(d, t), self.flat(d - d % 2 + core, chip)))
        return perm

    def back_perm(self, r):
        return [(dst, src) for src, dst in self.out_perm(r)]

    def group_perm(self, j):
        perm = []
        for d in range(self.dp):
            for t in range(self.parts):
                g = ((t % self.span) * 2 + d % 2) ^ j
                other = self.flat(d - d % 2 + g % 2, t - t % self.span + g // 2)
                perm.append((self.flat(d, t), other))
        return perm

    def xor_perm(self, dp_bits, z_bits):
        return [
            (self.flat(d, t), self.flat(d ^ dp_bits, t ^ z_bits))
            for d in range(self.dp)
            for t in range(self.parts)
        ]

    def fold_table(self):
        table = np.zeros((self.group, 2, self.parts), np.float32)
        for g in range(self.group):
            for q in range(self.parts):
                if g == 0:
                    table[g, :, q] = (1.0, (-1.0) ** q)
                else:
                    angle = 2.0 * math.pi * (q * g % self.parts) / self.parts
                    pair = (math.cos(angle), -math.sin(angle))
                    table[g, :, q] = [0.0 if abs(v) < 1e-9 else v for v in pair]
        return table


def whole(shape):
    return pl.BlockSpec(shape, lambda *_: (0,) * len(shape))


def once(shape):
    return pl.BlockSpec(shape, lambda *_: (0,) * len(shape), pipeline_mode=pl.Buffered(1))


SCALARS = pl.BlockSpec(memory_space=pltpu.SMEM)
LATER = pl.BlockSpec(memory_space=pl.ANY)


def params():
    return pltpu.CompilerParams(vmem_limit_bytes=VMEM_BYTES)


def block_order(plan, size):
    per = size // plan.parts
    return np.array([plan.parts * i + ka for pair in plan.pairs for ka in pair for i in range(per)])


def sort_kernel(plan, where, perm, value, *refs):
    outs = refs[-plan.parts :]
    per = perm.shape[0] // plan.parts
    for s in range(plan.seqs):
        rows = dot(perm[...], value[s].astype(LOW)).astype(LOW)
        for g in range(plan.group):
            piece = rows[g * 2 * per : (g + 1) * 2 * per].reshape(2, per, rows.shape[-1])
            r = (s * plan.group + g) ^ where[0]
            for k, out in enumerate(outs):

                @pl.when(r == k)
                def _(out=out, piece=piece):
                    out[...] = piece


def sort_rows(plan, where, value, after=()):
    seqs, rows, width = value.shape
    size = min(SORTED, rows)
    per = size // plan.parts
    order = block_order(plan, size)
    perm = jnp.asarray(order[:, None] == np.arange(size)[None, :], LOW)
    shape = jax.ShapeDtypeStruct((2, rows // plan.parts, width), LOW)
    return pl.pallas_call(
        functools.partial(sort_kernel, plan),
        grid=(rows // size,),
        in_specs=[SCALARS, whole((size, size)), pl.BlockSpec((seqs, size, width), lambda b: (0, b, 0))]
        + [LATER] * len(after),
        out_specs=[pl.BlockSpec((2, per, width), lambda b: (0, b, 0))] * plan.parts,
        out_shape=[shape] * plan.parts,
        compiler_params=params(),
        cost_estimate=LIGHT,
        name="sort_rows",
    )(where, perm, value, *after)


def unsorter(plan, size):
    return jnp.asarray(np.arange(size)[:, None] == block_order(plan, size)[None, :], LOW)


def unsort_kernel(plan, where, perm, *refs):
    blocks, out, rows = refs[: plan.parts], refs[-2], refs[-1]
    per = perm.shape[0] // plan.parts
    for s in range(plan.seqs):
        for g in range(plan.group):
            r = (s * plan.group + g) ^ where[0]
            for k, block in enumerate(blocks):

                @pl.when(r == k)
                def _(block=block, g=g):
                    rows[g * 2 * per : (g + 1) * 2 * per] = block[...].reshape(2 * per, rows.shape[-1])

        out[s] = dot(perm[...], rows[...])


def unsort_rows(plan, where, blocks):
    _, per_rows, width = blocks[0].shape
    rows = per_rows * plan.parts
    size = min(SORTED, rows)
    per = size // plan.parts
    perm = unsorter(plan, size)
    return pl.pallas_call(
        functools.partial(unsort_kernel, plan),
        grid=(rows // size,),
        in_specs=[SCALARS, whole((size, size))]
        + [pl.BlockSpec((2, per, width), lambda b: (0, b, 0))] * plan.parts,
        out_specs=pl.BlockSpec((plan.seqs, size, width), lambda b: (0, b, 0)),
        out_shape=jax.ShapeDtypeStruct((plan.seqs, rows, width), F32),
        scratch_shapes=[pltpu.VMEM((size, width), LOW)],
        compiler_params=params(),
        cost_estimate=LIGHT,
        name="unsort_rows",
    )(where, perm, *blocks)


def unsort_half_kernel(plan, half, where, perm, *refs):
    blocks, out, rows = refs[: plan.group], refs[-2], refs[-1]
    per = perm.shape[0] // plan.parts
    for g in range(plan.group):
        for k, block in enumerate(blocks):

            @pl.when((g ^ where[0]) % plan.group == k)
            def _(block=block, g=g):
                rows[g * 2 * per : (g + 1) * 2 * per] = block[...].reshape(2 * per, rows.shape[-1])

    out[0] = dot(perm[...], rows[...])


def unsort_half(plan, where, blocks, half, into=None):
    _, per_rows, width = blocks[0].shape
    rows = per_rows * plan.parts
    size = min(SORTED, rows)
    per = size // plan.parts
    perm = unsorter(plan, size)
    kept = [] if into is None else [into]
    return pl.pallas_call(
        functools.partial(unsort_half_kernel, plan, half),
        grid_spec=pltpu.PrefetchScalarGridSpec(
            num_scalar_prefetch=1,
            grid=(rows // size,),
            in_specs=[pl.BlockSpec((size, size), lambda b, where: (0, 0))]
            + [pl.BlockSpec((2, per, width), lambda b, where: (0, b, 0))] * plan.group
            + [LATER] * len(kept),
            out_specs=pl.BlockSpec(
                (1, size, width), lambda b, where: (where[0] // plan.group ^ half, b, 0)
            ),
            scratch_shapes=[pltpu.VMEM((size, width), LOW)],
        ),
        out_shape=jax.ShapeDtypeStruct((plan.seqs, rows, width), F32),
        input_output_aliases={2 + plan.group: 0} if kept else {},
        compiler_params=params(),
        cost_estimate=LIGHT,
        name="unsort_half",
    )(where, perm, *blocks, *kept)


def fold_kernel(plan, where, factors, *refs):
    parts, group = plan.parts, plan.group
    terms = [ref[0].astype(F32) for ref in refs[:parts]]
    outs, kept = refs[-1 - group : -1], refs[-1]
    for r in range(parts):
        kept[0, r] = refs[r][0]
    for j in range(group):
        for which in range(2):
            total = None
            for r in range(parts):
                place = ((where[2] ^ j) * 2 + which) * parts + (where[1] ^ r)
                term = factors[place] * terms[r]
                total = term if total is None else total + term
            outs[j][which] = total.astype(LOW)


def fold(plan, where, blocks, after=(), cost=LIGHT):
    parts = plan.parts
    _, per, width = blocks[0].shape
    step = min(256, per)
    steps = per // step
    stack = pl.BlockSpec((1, parts, step, width), lambda c, k: (c, 0, k, 0))
    single = pl.BlockSpec((1, step, width), lambda c, k: (c, k, 0))
    out = pl.BlockSpec((2, step, width), lambda c, k: (0, c * steps + k, 0))
    return pl.pallas_call(
        functools.partial(fold_kernel, plan),
        grid=(2, steps),
        in_specs=[SCALARS, SCALARS] + [single] * parts + [LATER] * len(after),
        out_specs=[out] * plan.group + [stack],
        out_shape=[jax.ShapeDtypeStruct((2, 2 * per, width), LOW)] * plan.group
        + [jax.ShapeDtypeStruct((2, parts, per, width), LOW)],
        compiler_params=params(),
        cost_estimate=cost,
        name="fold_parts",
    )(where, jnp.asarray(plan.fold_table().reshape(-1)), *blocks, *after)


def turn_waves(plan, where, pairs, wave, turned, step):
    first = jnp.where(where[2] == 0, 1.0, 0.0).astype(F32)
    rest = 1.0 - first
    width = wave.shape[0]
    own = pairs[0].shape[1]
    rows = own * plan.group
    for j, pair in enumerate(pairs):
        for k in range(own // step):
            span = slice(k * step, (k + 1) * step)
            pw = dot(pair[0, span], wave[...])
            qw = dot(pair[1, span], wave[...])
            pc, ps, qc, qs = pw[:, :width], pw[:, width:], qw[:, :width], qw[:, width:]
            at = j * own + k * step
            turned[0, at : at + step] = (pc + rest * qs).astype(LOW)
            turned[0, rows + at : rows + at + step] = (rest * qc - ps).astype(LOW)
            turned[1, at : at + step] = (first * qc + rest * (pc - qs)).astype(LOW)
            turned[1, rows + at : rows + at + step] = (-first * qs - rest * (qc + ps)).astype(LOW)


def normed(resid, gain, shift):
    centered = resid - jnp.mean(resid, axis=-1, keepdims=True)
    inverse = lax.rsqrt(jnp.mean(centered * centered, axis=-1, keepdims=True) + epsilon)
    scaled = centered * inverse
    return scaled * gain + shift, scaled, inverse


def forward_kernel(plan, where, *refs):
    group, parts = plan.group, plan.parts
    pairs, refs = refs[:group], refs[group:]
    (wave, cos_rows, sin_rows, taken, b_in, vectors, *refs) = refs
    (w_in, w_out), refs, copies = split_weights(plan, where, refs)
    acts, (low_out, one_out, two_out, scales, hidden_out, slope_out, turned) = refs[:parts], refs[parts:]
    c, r = pl.program_id(0), pl.program_id(1)
    _, many, per, width = taken.shape
    rows = many * per

    @pl.when((c == 0) & (r == 0))
    def _():
        for copy in copies():
            copy.start()
        turn_waves(plan, where, pairs, wave, turned, min(256, pairs[0].shape[1]))
        for copy in copies():
            copy.wait()

    mixed = section(cos_rows, sin_rows, turned, c)
    b_out, gain_one, shift_one, gain_two, shift_two = (vectors[k : k + 1] for k in range(5))
    resid = taken[0].reshape(rows, width).astype(F32) + mixed
    normed_one, scaled_one, inverse_one = normed(resid, gain_one, shift_one)
    low = normed_one.astype(LOW)
    low_out[0] = low.reshape(many, per, width)
    one_out[0] = scaled_one.astype(LOW).reshape(many, per, width)
    branch = normed_one + b_out
    for h in range(parts):
        pre = dot(low, w_in[h]) + b_in[h : h + 1]
        square = pre * pre
        bend = jnp.tanh(pre * (GELU_C + (GELU_C * GELU_A) * square))
        half = 0.5 * pre
        hidden = (half + half * bend).astype(LOW)
        slope = 0.5 + 0.5 * bend + half * (1.0 - bend * bend) * (GELU_C + (3.0 * GELU_C * GELU_A) * square)
        hidden_out[0, :, h] = hidden.reshape(many, per, hidden.shape[1])
        slope_out[0, :, h] = slope.astype(LOW).reshape(many, per, hidden.shape[1])
        branch = branch + dot(hidden, w_out[h])
    normed_two, scaled_two, inverse_two = normed(branch, gain_two, shift_two)
    two_out[0] = scaled_two.astype(LOW).reshape(many, per, width)
    lanes = lax.broadcasted_iota(jnp.int32, (rows, 128), 1)
    scales[0] = jnp.where(lanes == 0, inverse_one, inverse_two).reshape(many, per, 128)
    act = normed_two.astype(LOW)
    for k in range(parts):

        @pl.when(r == k // many)
        def _(k=k):
            acts[k][0] = act[k % many * per : (k % many + 1) * per]


def section(cos_rows, sin_rows, turned, c):
    rows = cos_rows.shape[2]
    return dot(cos_rows[0], turned[c, :rows]) + dot(sin_rows[0], turned[c, rows:])


def weight_specs(plan, weights):
    return [LATER if plan.slabs else once(w.shape) for w in weights]


def weight_scratch(plan, weights):
    if not plan.slabs:
        return []
    chunks, slab, hid = weights[0].shape
    return [
        pltpu.VMEM((chunks, slab * len(weights), hid), LOW),
        pltpu.SemaphoreType.DMA((len(weights),)),
    ]


def slab_copies(plan, where, slabs, room, sems):
    slab = slabs[0].shape[1]
    for j, ref in enumerate(slabs):
        at = pl.multiple_of((where[4] ^ j) * slab, 16)
        yield pltpu.make_async_copy(ref, room.at[:, pl.ds(at, slab)], sems.at[j])


def split_weights(plan, where, refs):
    if plan.slabs:
        slabs, refs, room, sems = refs[: plan.dp], refs[plan.dp : -2], refs[-2], refs[-1]

        def copies():
            return slab_copies(plan, where, slabs, room, sems)

        return (room.at[: plan.parts], room.at[plan.parts :]), refs, copies
    return refs[:2], refs[2:], lambda: ()


def forward(plan, where, pairs, wave, tables, taken, b_in, vectors, weights):
    parts = plan.parts
    _, _, per, width = taken.shape
    rows = per * parts
    hid = b_in.shape[1]
    many = 1
    tile = pl.BlockSpec((1, many, per, width), lambda c, r: (c, r, 0, 0))
    wide = pl.BlockSpec((1, many, parts, per, hid), lambda c, r: (c, r, 0, 0, 0))
    low = jax.ShapeDtypeStruct((2, parts, per, width), LOW)
    big = jax.ShapeDtypeStruct((2, parts, parts, per, hid), LOW)
    return pl.pallas_call(
        functools.partial(forward_kernel, plan),
        grid=(2, parts // many),
        in_specs=[SCALARS]
        + [once(pairs[0].shape)] * plan.group
        + [
            once(wave.shape),
            pl.BlockSpec((1, many * per, rows), lambda c, r: (c, r, 0)),
            pl.BlockSpec((1, many * per, rows), lambda c, r: (c, r, 0)),
            tile,
            once(b_in.shape),
            once(vectors.shape),
        ]
        + weight_specs(plan, weights),
        out_specs=[pl.BlockSpec((1, per, width), lambda c, r: (c, 0, 0))] * parts
        + [tile, tile, tile, pl.BlockSpec((1, many, per, 128), lambda c, r: (c, r, 0, 0)), wide, wide],
        out_shape=[jax.ShapeDtypeStruct((2, per, width), LOW)] * parts
        + [low, low, low, jax.ShapeDtypeStruct((2, parts, per, 128), F32), big, big],
        scratch_shapes=[pltpu.VMEM((2, 2 * rows, width), LOW)] + weight_scratch(plan, weights),
        compiler_params=params(),
        cost_estimate=LIGHT,
        name="mix_forward",
    )(where, *pairs, wave, *tables, taken, b_in, vectors, *weights)


def norm_back(grad, scaled, inverse, gain):
    grad_scaled = grad * gain
    return inverse * (
        grad_scaled
        - jnp.mean(grad_scaled, axis=-1, keepdims=True)
        - scaled * jnp.mean(grad_scaled * scaled, axis=-1, keepdims=True)
    )


def column_sum(value):
    return jnp.sum(value, axis=0, keepdims=True)


def backward_kernel(plan, tiles, where, factors, *refs):
    parts, group = plan.parts, plan.group
    cotangents, refs = refs[:parts], refs[parts:]
    (two, scales_two, low, hidden, slope, one, scales_one, vectors, *refs) = refs
    (w_in, w_out), refs, copies = split_weights(plan, where, refs)
    (first_out, sums, bias, *refs) = refs
    folded, halves, refs = refs[:group], refs[group : group + 4], refs[group + 4 :]
    (grad_in, grad_out, cotangent, coming, coming_low, branch, total, leaving, rounded, *refs) = refs
    stages, sems = refs[:4], refs[4]
    step = pl.program_id(0)
    gain_one, gain_two = vectors[1:2], vectors[3:4]
    half = grad_in.shape[1] // 2

    def norm_two():
        r = lax.rem(step, parts)
        for k in range(parts):

            @pl.when(r == k)
            def _(k=k):
                cotangent[...] = cotangents[k][0]

    def stage_two():
        grad = cotangent[...].astype(F32)
        scaled = two[0, 0].astype(F32)
        second = norm_back(grad, scaled, scales_two[0, 0, :, 1:2], gain_two)
        second_low = second.astype(LOW)
        sums[2:3] += column_sum(grad * scaled)
        sums[3:4] += column_sum(grad)
        sums[4:5] += column_sum(second_low.astype(F32))
        coming[...] = second
        coming_low[...] = second_low

    def turn_over():
        leaving[...] = total[...]
        total[...] = coming[...]
        branch[...] = coming_low[...]

    def feed(last):
        low_turned = low[0, 0].T
        branch_turned = branch[...].T
        for h in range(parts):
            pre = (dot_nt(branch[...], w_out[h]) * slope[0, 0, h].astype(F32)).astype(LOW)
            bias[h : h + 1] += column_sum(pre.astype(F32))
            total[...] += dot_nt(pre, w_in[h])
            grads = (dot(low_turned, pre), dot(branch_turned, hidden[0, 0, h]))
            if not last:
                grad_in[h] += grads[0]
                grad_out[h] += grads[1]
                continue
            for k, (kept, grad) in enumerate(zip((grad_in, grad_out), grads)):
                grad = (kept[h] + grad).astype(LOW)
                stages[2 * k][h] = jnp.where(where[3] == 0, grad[:half], grad[half:])
                stages[2 * k + 1][h] = jnp.where(where[3] == 0, grad[half:], grad[:half])
            for k in range(4):
                pltpu.make_async_copy(stages[k].at[h], halves[k].at[h], sems.at[k, h]).start()

    def norm_one(valid):
        back = jnp.where(valid, leaving[...], 0.0)
        scaled = one[0, 0].astype(F32)
        first = norm_back(back, scaled, scales_one[0, 0, :, 0:1], gain_one)
        sums[0:1] += column_sum(back * scaled)
        sums[1:2] += column_sum(back)
        first_out[0, 0] = first
        rounded[lax.rem(jnp.maximum(step - 2, 0), parts)] = first.astype(LOW)

    def fold_all():
        for j in range(group):
            for which in range(2):
                value = None
                for r in range(parts):
                    place = ((where[2] ^ j) * 2 + which) * parts + (where[1] ^ r)
                    term = factors[place] * rounded[r].astype(F32)
                    value = term if value is None else value + term
                folded[j][which] = value.astype(LOW)

    @pl.when(step == 0)
    def _():
        for copy in copies():
            copy.start()
        sums[...] = jnp.zeros_like(sums)
        bias[...] = jnp.zeros_like(bias)
        grad_in[...] = jnp.zeros_like(grad_in)
        grad_out[...] = jnp.zeros_like(grad_out)

    @pl.when(step < tiles)
    def _():
        norm_two()

    @pl.when(step == 0)
    def _():
        stage_two()
        for copy in copies():
            copy.wait()

    @pl.when((step > 0) & (step < tiles))
    def _():
        turn_over()
        stage_two()
        feed(False)
        norm_one(step > 1)

    @pl.when(step == tiles)
    def _():
        turn_over()
        feed(True)
        norm_one(True)

    @pl.when(step == tiles + 1)
    def _():
        leaving[...] = total[...]
        norm_one(True)

    @pl.when((step > 1) & (lax.rem(step - 1, parts) == 0))
    def _():
        fold_all()

    @pl.when(step == tiles + 1)
    def _():
        for k in range(4):
            for h in range(parts):
                pltpu.make_async_copy(stages[k].at[h], halves[k].at[h], sems.at[k, h]).wait()


def backward(plan, where, cotangents, low, one, two, scales, hidden, slope, vectors, weights):
    parts, group = plan.parts, plan.group
    _, _, per, width = low.shape
    hid = hidden.shape[-1]
    tiles = 2 * parts

    def tile(lag, *rest):
        def place(s):
            at = jnp.clip(s - lag, 0, tiles - 1)
            return (at // parts, at % parts) + (0,) * len(rest)

        return pl.BlockSpec((1, 1, *rest), place)

    def class_of(lag):
        return lambda s: jnp.clip(s - lag, 0, tiles - 1) // parts

    half = jax.ShapeDtypeStruct((parts, width // 2, hid), LOW)
    return pl.pallas_call(
        functools.partial(backward_kernel, plan, tiles),
        grid=(tiles + 2,),
        in_specs=[SCALARS, SCALARS]
        + [pl.BlockSpec((1, per, width), lambda s: (class_of(0)(s), 0, 0))] * parts
        + [
            tile(0, per, width),
            tile(0, per, 128),
            tile(1, per, width),
            tile(1, parts, per, hid),
            tile(1, parts, per, hid),
            tile(2, per, width),
            tile(2, per, 128),
            once(vectors.shape),
        ]
        + weight_specs(plan, weights),
        out_specs=[tile(2, per, width), once((8, width)), once((parts, hid))]
        + [pl.BlockSpec((2, per, width), lambda s: (0, class_of(2)(s), 0))] * group
        + [LATER] * 4,
        out_shape=[
            jax.ShapeDtypeStruct((2, parts, per, width), F32),
            jax.ShapeDtypeStruct((8, width), F32),
            jax.ShapeDtypeStruct((parts, hid), F32),
        ]
        + [jax.ShapeDtypeStruct((2, 2 * per, width), LOW)] * group
        + [half] * 4,
        scratch_shapes=[
            pltpu.VMEM((parts, width, hid), F32),
            pltpu.VMEM((parts, width, hid), F32),
            pltpu.VMEM((per, width), LOW),
            pltpu.VMEM((per, width), F32),
            pltpu.VMEM((per, width), LOW),
            pltpu.VMEM((per, width), LOW),
            pltpu.VMEM((per, width), F32),
            pltpu.VMEM((per, width), F32),
            pltpu.VMEM((parts, per, width), LOW),
        ]
        + [pltpu.VMEM(half.shape, LOW)] * 4
        + [pltpu.SemaphoreType.DMA((4, parts))]
        + weight_scratch(plan, weights),
        compiler_params=params(),
        cost_estimate=LONG,
        name="feed_backward",
    )(
        where,
        jnp.asarray(plan.fold_table().reshape(-1)),
        *cotangents,
        two,
        scales,
        low,
        hidden,
        slope,
        one,
        scales,
        vectors,
        *weights,
    )


def mix_back_kernel(plan, where, *refs):
    group = plan.group
    pairs, (wave, cos_rows, sin_rows, first), outs, turned = (
        refs[:group],
        refs[group : group + 4],
        refs[-1 - group : -1],
        refs[-1],
    )
    c, r = pl.program_id(0), pl.program_id(1)
    _, many, per, width = first.shape

    @pl.when((c == 0) & (r == 0))
    def _():
        turn_waves(plan, where, pairs, wave, turned, min(256, pairs[0].shape[1]))

    total = first[0].reshape(many * per, width) + section(cos_rows, sin_rows, turned, c)
    total = total.astype(LOW)
    for k in range(group):

        @pl.when(r == k // many)
        def _(k=k):
            outs[k][0] = total[k % many * per : (k % many + 1) * per]


def mix_back(plan, where, pairs, wave, tables, first, half, after=(), cost=LIGHT):
    parts, group = plan.parts, plan.group
    _, _, per, width = first.shape
    rows = per * parts
    many = 2
    begin = half * group // many
    return pl.pallas_call(
        functools.partial(mix_back_kernel, plan),
        grid=(2, group // many),
        in_specs=[SCALARS]
        + [once(pairs[0].shape)] * group
        + [
            once(wave.shape),
            pl.BlockSpec((1, many * per, rows), lambda c, r: (c, begin + r, 0)),
            pl.BlockSpec((1, many * per, rows), lambda c, r: (c, begin + r, 0)),
            pl.BlockSpec((1, many, per, width), lambda c, r: (c, begin + r, 0, 0)),
        ]
        + [LATER] * len(after),
        out_specs=[pl.BlockSpec((1, per, width), lambda c, r: (c, 0, 0))] * group,
        out_shape=[jax.ShapeDtypeStruct((2, per, width), LOW)] * group,
        scratch_shapes=[pltpu.VMEM((2, 2 * rows, width), LOW)],
        compiler_params=params(),
        cost_estimate=cost,
        name="mix_backward",
    )(where, *pairs, wave, *tables, first, *after)


def add_split_kernel(bits, *refs):
    for k in range(2):
        one, two, keep, give = refs[2 * k], refs[2 * k + 1], refs[4 + 2 * k], refs[5 + 2 * k]
        total = (one[...].astype(F32) + two[...].astype(F32)).astype(LOW)
        half = keep.shape[1]
        low_half, high_half = total[:, :half], total[:, half:]
        keep[...] = jnp.where(bits[k] == 0, low_half, high_half)
        give[...] = jnp.where(bits[k] == 0, high_half, low_half)


def add_split(bits, pairs, cost):
    chunks, rows, hid = pairs[0][0].shape
    block = pl.BlockSpec((1, rows, hid), lambda h: (h, 0, 0))
    half = pl.BlockSpec((1, rows // 2, hid), lambda h: (h, 0, 0))
    outs = pl.pallas_call(
        add_split_kernel,
        grid=(chunks,),
        in_specs=[SCALARS] + [block] * 4,
        out_specs=[half] * 4,
        out_shape=[jax.ShapeDtypeStruct((chunks, rows // 2, hid), LOW)] * 4,
        compiler_params=params(),
        cost_estimate=cost,
        name="add_split",
    )(bits, *pairs[0], *pairs[1])
    return [outs[:2], outs[2:]]


def add_spread_kernel(order, *refs):
    for k in range(2):
        total = (refs[2 * k][...].astype(F32) + refs[2 * k + 1][...].astype(F32)).astype(LOW)
        for at, chunk in enumerate(order):
            refs[4 + chunk][k] = total[at]


def add_spread(order, pairs):
    chunks, rows, hid = pairs[0][0].shape
    block = pl.BlockSpec((chunks, rows, hid), lambda: (0, 0, 0))
    return pl.pallas_call(
        functools.partial(add_spread_kernel, order),
        in_specs=[block] * 4,
        out_specs=[pl.BlockSpec((2, rows, hid), lambda: (0, 0, 0))] * chunks,
        out_shape=[jax.ShapeDtypeStruct((2, rows, hid), LOW)] * chunks,
        compiler_params=params(),
        cost_estimate=LIGHT,
        name="add_spread",
    )(*pairs[0], *pairs[1])


def add_all_kernel(*refs):
    total = refs[0][...].astype(F32)
    for ref in refs[1:-1]:
        total = total + ref[...].astype(F32)
    refs[-1][...] = total.astype(LOW)


def add_all(values):
    block = pl.BlockSpec(values[0].shape, lambda: (0, 0, 0))
    return pl.pallas_call(
        add_all_kernel,
        in_specs=[block] * len(values),
        out_specs=block,
        out_shape=jax.ShapeDtypeStruct(values[0].shape, LOW),
        compiler_params=params(),
        cost_estimate=LIGHT,
        name="add_all",
    )(*values)


def finish_kernel(places, *refs):
    blocks, (grad_in, grad_out, rows) = refs[:-3], refs[-3:]
    slab = blocks[0].shape[1]
    for j, block in enumerate(blocks):
        for k, out in enumerate((grad_in, rows)):
            at = pl.multiple_of(places[k * len(blocks) + j] * slab, 8)
            out[pl.ds(at, slab)] = block[k].astype(F32)
    grad_out[...] = rows[...].T


def finish(places, blocks):
    _, slab, hid = blocks[0].shape
    width = slab * len(blocks)
    step = math.gcd(hid, 256)
    return pl.pallas_call(
        finish_kernel,
        grid=(hid // step,),
        in_specs=[SCALARS] + [pl.BlockSpec((2, slab, step), lambda h: (0, 0, h))] * len(blocks),
        out_specs=[
            pl.BlockSpec((width, step), lambda h: (0, h)),
            pl.BlockSpec((step, width), lambda h: (h, 0)),
        ],
        out_shape=[
            jax.ShapeDtypeStruct((width, hid), F32),
            jax.ShapeDtypeStruct((hid, width), F32),
        ],
        scratch_shapes=[pltpu.VMEM((width, step), F32)],
        compiler_params=params(),
        cost_estimate=LIGHT,
        name="finish_weights",
    )(places, *blocks)


def angle_pair(steps, modulus):
    angle = (2.0 * math.pi / modulus) * (steps % modulus).astype(F32)
    return jnp.cos(angle), jnp.sin(angle)


def product_tables(coarse, fine, modulus, shape):
    cos_a, sin_a = angle_pair(coarse, modulus)
    cos_b, sin_b = angle_pair(fine, modulus)
    cos = (cos_a * cos_b - sin_a * sin_b).astype(LOW)
    sin = (sin_a * cos_b + cos_a * sin_b).astype(LOW)
    return cos.reshape(shape), sin.reshape(shape)


def width_table(index):
    width = index.shape[0]
    coarse = jnp.arange(width // 32, dtype=jnp.int32) * 32
    fine = jnp.arange(32, dtype=jnp.int32)
    pair = product_tables(
        (coarse[:, None] * index)[:, None, :], (fine[:, None] * index)[None], width, (width, width)
    )
    return jnp.concatenate(pair, axis=1)


def section_table(plan, g, b, rows):
    parts, group = plan.parts, plan.group
    length, per = rows * parts, rows // parts
    classes = jnp.asarray(plan.pairs, jnp.int32)
    steps = jnp.arange(per, dtype=jnp.int32)
    mine = lax.dynamic_index_in_dim(classes, g, 0, keepdims=False)
    cols = jnp.concatenate(
        [
            (lax.dynamic_index_in_dim(classes, g ^ j, 0, keepdims=False)[:, None] + parts * steps).reshape(-1)
            for j in range(group)
        ]
    )
    fine = jnp.arange(32, dtype=jnp.int32)
    coarse = jnp.concatenate([per * (b ^ r) + 32 * jnp.arange(per // 32, dtype=jnp.int32) for r in range(parts)])
    first = ((parts * coarse + mine[:, None])[:, :, None] * cols)[:, :, None, :]
    second = (parts * fine[:, None] * cols)[None, None]
    return product_tables(first, second, length, (2, rows, rows))


def body(plan, tokens, w_in, b_in, w_out, b_out, gain_one, shift_one, gain_two, shift_two, out_grad):
    seqs, rows, width = tokens.shape
    parts, group = plan.parts, plan.group
    hid = w_in.shape[1]
    d = lax.axis_index("dp")
    t = lax.axis_index("tensor")
    g = (t % plan.span) * 2 + d % 2
    b = (t // plan.span) % seqs * group + g
    where = jnp.stack([t, b, g, d % 2, d]).astype(jnp.int32)

    def permute(value, perm):
        return lax.ppermute(value, BOTH, perm)

    def tie(values, *after):
        return lax.optimization_barrier((*values, *after))[: len(values)]

    def over_pairs(own):
        blocks = {0: own}
        for j in range(2, plan.dp, 2):
            blocks[j] = permute(own, plan.xor_perm(j, 0))
        for j in range(0, plan.dp, 2):
            blocks[j + 1] = permute(blocks[j], plan.xor_perm(1, 0))
        return [blocks[j] for j in range(plan.dp)]

    z_bits = [1 << k for k in range(parts.bit_length() - 1)]
    slab_in, slab_out = width // plan.dp, hid // plan.dp
    flat_in = slab_in * hid // width
    packed = jnp.concatenate(
        [
            lax.dynamic_slice_in_dim(w_in, d * slab_in, slab_in, 0).reshape(flat_in, width),
            lax.dynamic_slice_in_dim(w_out, d * slab_out, slab_out, 0),
            jnp.pad(b_in[None], ((0, 15), (0, width - hid))),
        ]
    )
    sorted_tokens = sort_rows(plan, where, tokens)
    slabs, z_order = packed[None], [0]
    for bit in reversed(z_bits):
        z_order += [other ^ bit for other in z_order]
        slabs = jnp.concatenate([slabs, permute(slabs, plan.xor_perm(0, bit))])
        if bit == z_bits[-1]:
            slabs, *sorted_tokens = tie([slabs, *sorted_tokens])
    taken_blocks = [permute(block, plan.out_perm(r)) for r, block in enumerate(sorted_tokens)]

    bias_in = slabs[:, flat_in + slab_out, :hid].astype(F32)
    slabs_in = slabs[:, :flat_in].reshape(parts, slab_in, hid)
    slabs_out = slabs[:, flat_in : flat_in + slab_out]
    plan.slabs = slabs_in.shape == slabs_out.shape and slab_in % 16 == 0
    if plan.slabs:
        weights = over_pairs(tie([jnp.concatenate([slabs_in, slabs_out])], taken_blocks[0])[0])
    else:
        weights = [lax.all_gather(value, "dp", axis=1, tiled=True) for value in (slabs_in, slabs_out)]

    vectors = jnp.stack([b_out, gain_one, shift_one, gain_two, shift_two])
    late_g, late_b, index = tie([g, b, jnp.arange(width, dtype=jnp.int32)], taken_blocks[0])
    wave = width_table(index)
    tables = section_table(plan, late_g, late_b, rows)

    def send_back(blocks):
        return [permute(block, plan.back_perm(r)) for r, block in enumerate(blocks)]

    def exchange(folded):
        return [folded[0]] + [permute(folded[j], plan.group_perm(j)) for j in range(1, group)]

    sorted_grad = sort_rows(plan, where, out_grad, taken_blocks[:1])
    *folded, taken = fold(
        plan, where, taken_blocks, (wave, *tables, bias_in, vectors, sorted_grad[0], *weights[1:2]), LONG
    )
    sorted_grad = tie(sorted_grad, *taken_blocks)
    cotangents = [permute(block, plan.out_perm(r)) for r, block in enumerate(sorted_grad)]

    outs = forward(plan, where, exchange(folded), wave, tables, taken, bias_in, vectors, weights)
    acts, saved = send_back(outs[:parts]), outs[parts:]

    first, sums, bias, *rest = backward(plan, where, cotangents, *saved, vectors, weights)
    folded, halves = rest[:group], rest[group:]

    bits = [1 << k for k in range(plan.dp.bit_length() - 1)]
    orders = (bits, bits[:1] + bits[:0:-1])

    def bits_of(step):
        return jnp.stack([(d // order[step]) % 2 for order in orders]).astype(jnp.int32)

    def swap(pairs, step):
        return [
            (keep, permute(give, plan.xor_perm(order[step], 0)))
            for (keep, give), order in zip(pairs, orders)
        ]

    def tie_pairs(pairs, *after):
        flat = tie([x for pair in pairs for x in pair], *after)
        return [flat[:2], flat[2:]]

    def tree(values):
        while len(values) > 1:
            values = [one + two for one, two in zip(values[::2], values[1::2])]
        return values[0]

    folded = tie(folded, *acts)
    exchanged = exchange(folded)
    grad_blocks = list(mix_back(plan, where, exchanged, wave, tables, first, 0))
    halves = tie(halves, *exchanged)
    pairs = tie_pairs(swap([halves[:2], halves[2:]], 0), grad_blocks[0])
    halves = add_split(bits_of(1), pairs, LIGHT)
    flat = [x for pair in halves for x in pair]
    grad_blocks += mix_back(plan, where, exchanged, wave, tables, first, 1, flat, LONG)

    returned = []

    def give_back(r, *after):
        block = tie([grad_blocks[r]], *after)[0] if after else grad_blocks[r]
        returned.append(permute(block, plan.back_perm(r)))

    for r in range(group):
        give_back(r)
    activations = unsort_rows(plan, where, tie(acts, grad_blocks[-1]))
    for k in range(1, len(bits) - 1):
        halves = add_split(bits_of(k + 1), tie_pairs(swap(halves, k), activations), LIGHT)
    for r in range(group, parts - 1):
        give_back(r, *returned[:group], activations)
    input_grad = unsort_half(plan, where, returned[:group], 0)
    small = tie([jnp.concatenate([sums[:5], bias.reshape(-1, width)])], input_grad)[0]
    for bit in bits:
        small = small + permute(small, plan.xor_perm(bit, 0))
    pairs = tie_pairs(swap(halves, len(bits) - 1), activations, small, *returned)
    chunks = add_spread(z_order, pairs)

    values = [chunks[0]] + [permute(chunks[k], plan.xor_perm(0, k)) for k in range(1, parts)]
    flat_sums, bias = small[:5].reshape(-1), small[5:].reshape(parts, hid)
    pads = [jnp.concatenate([flat_sums, bias[z_order.index(k)]]) for k in range(parts)]
    pads = tie(pads, chunks[0])
    got = [pads[0]] + [permute(pads[k], plan.xor_perm(0, k)) for k in range(1, parts)]
    small = tree(got)
    give_back(parts - 1, *values, small)
    total = add_all(values)
    blocks = {0: total}
    for j in range(2, plan.dp, 2):
        blocks[j] = permute(total, plan.xor_perm(j, 0))
    input_grad = unsort_half(plan, where, returned[group:], 1, input_grad)
    blocks[plan.dp - 2] = tie([blocks[plan.dp - 2]], input_grad)[0]
    for j in range(0, plan.dp, 2):
        blocks[j + 1] = permute(blocks[j], plan.xor_perm(1, 0))
    blocks = [blocks[j] for j in range(plan.dp)]
    places = [
        sum((((d ^ j) // bit) % 2) * (plan.dp >> k + 1) for k, bit in enumerate(order))
        for order in orders
        for j in range(plan.dp)
    ]
    grad_w_in, grad_w_out = finish(jnp.stack(places).astype(jnp.int32), blocks)
    return (
        activations,
        input_grad,
        grad_w_in,
        small[5 * width :],
        grad_w_out,
        *(small[k * width : (k + 1) * width] for k in (4, 0, 1, 2, 3)),
    )


def solution(mesh):
    def shards(tokens, *rest):
        return body(Plan(mesh, tokens.shape[0]), tokens, *rest)

    rows = P("dp", "tensor", None)
    return jax.shard_map(
        shards,
        mesh=mesh,
        in_specs=(rows, P(None, "tensor"), P("tensor"), P("tensor", None), P(), P(), P(), P(), P(), rows),
        out_specs=(rows, rows, P(None, "tensor"), P("tensor"), P("tensor", None), P(), P(), P(), P(), P()),
        check_vma=False,
    )
```

```python
import functools
import math

import jax
import jax.numpy as jnp
import numpy as np
from jax import lax
from jax.experimental import pallas as pl
from jax.experimental.pallas import tpu as pltpu
from jax.sharding import PartitionSpec as P

epsilon = 1e-12
LOW = jnp.bfloat16
F32 = jnp.float32
BOTH = ("dp", "tensor")
SORTED = 256
VMEM_BYTES = 60 * 1024 * 1024
LONG = pl.CostEstimate(flops=3 * 10**11, bytes_accessed=1 << 20, transcendentals=0)
LIGHT = pl.CostEstimate(flops=1024, bytes_accessed=1024, transcendentals=0)
GELU_C = math.sqrt(2.0 / math.pi)
GELU_A = 0.044715


def dot(left, right):
    return lax.dot_general(left, right, (((1,), (0,)), ((), ())), preferred_element_type=F32)


def dot_nt(left, right):
    return lax.dot_general(left, right, (((1,), (1,)), ((), ())), preferred_element_type=F32)


class Plan:
    def __init__(self, mesh, seqs):
        self.dp = mesh.shape["dp"]
        self.parts = mesh.shape["tensor"]
        self.seqs = seqs
        self.group = self.parts // seqs
        self.span = self.group // 2
        assert seqs == 2 and self.group >= 2 and self.parts & (self.parts - 1) == 0
        assert self.dp & (self.dp - 1) == 0
        self.pairs = [(0, self.group)] + [(g, self.parts - g) for g in range(1, self.group)]

    def flat(self, d, t):
        return d * self.parts + t

    def owner(self, core, block):
        seq, g = divmod(block, self.group)
        return g % 2, (core * self.seqs + seq) * self.span + g // 2

    def out_perm(self, r):
        perm = []
        for d in range(self.dp):
            for t in range(self.parts):
                core, chip = self.owner(d % 2, t ^ r)
                perm.append((self.flat(d, t), self.flat(d - d % 2 + core, chip)))
        return perm

    def back_perm(self, r):
        return [(dst, src) for src, dst in self.out_perm(r)]

    def group_perm(self, j):
        perm = []
        for d in range(self.dp):
            for t in range(self.parts):
                g = ((t % self.span) * 2 + d % 2) ^ j
                other = self.flat(d - d % 2 + g % 2, t - t % self.span + g // 2)
                perm.append((self.flat(d, t), other))
        return perm

    def xor_perm(self, dp_bits, z_bits):
        return [
            (self.flat(d, t), self.flat(d ^ dp_bits, t ^ z_bits))
            for d in range(self.dp)
            for t in range(self.parts)
        ]

    def fold_table(self):
        table = np.zeros((self.group, 2, self.parts), np.float32)
        for g in range(self.group):
            for q in range(self.parts):
                if g == 0:
                    table[g, :, q] = (1.0, (-1.0) ** q)
                else:
                    angle = 2.0 * math.pi * (q * g % self.parts) / self.parts
                    pair = (math.cos(angle), -math.sin(angle))
                    table[g, :, q] = [0.0 if abs(v) < 1e-9 else v for v in pair]
        return table


def whole(shape):
    return pl.BlockSpec(shape, lambda *_: (0,) * len(shape))


def once(shape):
    return pl.BlockSpec(shape, lambda *_: (0,) * len(shape), pipeline_mode=pl.Buffered(1))


SCALARS = pl.BlockSpec(memory_space=pltpu.SMEM)
LATER = pl.BlockSpec(memory_space=pl.ANY)


def params():
    return pltpu.CompilerParams(vmem_limit_bytes=VMEM_BYTES)


def block_order(plan, size):
    per = size // plan.parts
    return np.array([plan.parts * i + ka for pair in plan.pairs for ka in pair for i in range(per)])


def sort_kernel(plan, where, perm, value, *refs):
    outs = refs[-plan.parts :]
    per = perm.shape[0] // plan.parts
    for s in range(plan.seqs):
        rows = dot(perm[...], value[s].astype(LOW)).astype(LOW)
        for g in range(plan.group):
            piece = rows[g * 2 * per : (g + 1) * 2 * per].reshape(2, per, rows.shape[-1])
            r = (s * plan.group + g) ^ where[0]
            for k, out in enumerate(outs):

                @pl.when(r == k)
                def _(out=out, piece=piece):
                    out[...] = piece


def sort_rows(plan, where, value, after=()):
    seqs, rows, width = value.shape
    size = min(SORTED, rows)
    per = size // plan.parts
    order = block_order(plan, size)
    perm = jnp.asarray(order[:, None] == np.arange(size)[None, :], LOW)
    shape = jax.ShapeDtypeStruct((2, rows // plan.parts, width), LOW)
    return pl.pallas_call(
        functools.partial(sort_kernel, plan),
        grid=(rows // size,),
        in_specs=[SCALARS, whole((size, size)), pl.BlockSpec((seqs, size, width), lambda b: (0, b, 0))]
        + [LATER] * len(after),
        out_specs=[pl.BlockSpec((2, per, width), lambda b: (0, b, 0))] * plan.parts,
        out_shape=[shape] * plan.parts,
        compiler_params=params(),
        cost_estimate=LIGHT,
        name="sort_rows",
    )(where, perm, value, *after)


def unsorter(plan, size):
    return jnp.asarray(np.arange(size)[:, None] == block_order(plan, size)[None, :], LOW)


def unsort_kernel(plan, where, perm, *refs):
    blocks, out, rows = refs[: plan.parts], refs[-2], refs[-1]
    per = perm.shape[0] // plan.parts
    for s in range(plan.seqs):
        for g in range(plan.group):
            r = (s * plan.group + g) ^ where[0]
            for k, block in enumerate(blocks):

                @pl.when(r == k)
                def _(block=block, g=g):
                    rows[g * 2 * per : (g + 1) * 2 * per] = block[...].reshape(2 * per, rows.shape[-1])

        out[s] = dot(perm[...], rows[...])


def unsort_rows(plan, where, blocks):
    _, per_rows, width = blocks[0].shape
    rows = per_rows * plan.parts
    size = min(SORTED, rows)
    per = size // plan.parts
    perm = unsorter(plan, size)
    return pl.pallas_call(
        functools.partial(unsort_kernel, plan),
        grid=(rows // size,),
        in_specs=[SCALARS, whole((size, size))]
        + [pl.BlockSpec((2, per, width), lambda b: (0, b, 0))] * plan.parts,
        out_specs=pl.BlockSpec((plan.seqs, size, width), lambda b: (0, b, 0)),
        out_shape=jax.ShapeDtypeStruct((plan.seqs, rows, width), F32),
        scratch_shapes=[pltpu.VMEM((size, width), LOW)],
        compiler_params=params(),
        cost_estimate=LIGHT,
        name="unsort_rows",
    )(where, perm, *blocks)


def unsort_half_kernel(plan, half, where, perm, *refs):
    blocks, out, rows = refs[: plan.group], refs[-2], refs[-1]
    per = perm.shape[0] // plan.parts
    for g in range(plan.group):
        for k, block in enumerate(blocks):

            @pl.when((g ^ where[0]) % plan.group == k)
            def _(block=block, g=g):
                rows[g * 2 * per : (g + 1) * 2 * per] = block[...].reshape(2 * per, rows.shape[-1])

    out[0] = dot(perm[...], rows[...])


def unsort_half(plan, where, blocks, half, into=None):
    _, per_rows, width = blocks[0].shape
    rows = per_rows * plan.parts
    size = min(SORTED, rows)
    per = size // plan.parts
    perm = unsorter(plan, size)
    kept = [] if into is None else [into]
    return pl.pallas_call(
        functools.partial(unsort_half_kernel, plan, half),
        grid_spec=pltpu.PrefetchScalarGridSpec(
            num_scalar_prefetch=1,
            grid=(rows // size,),
            in_specs=[pl.BlockSpec((size, size), lambda b, where: (0, 0))]
            + [pl.BlockSpec((2, per, width), lambda b, where: (0, b, 0))] * plan.group
            + [LATER] * len(kept),
            out_specs=pl.BlockSpec(
                (1, size, width), lambda b, where: (where[0] // plan.group ^ half, b, 0)
            ),
            scratch_shapes=[pltpu.VMEM((size, width), LOW)],
        ),
        out_shape=jax.ShapeDtypeStruct((plan.seqs, rows, width), F32),
        input_output_aliases={2 + plan.group: 0} if kept else {},
        compiler_params=params(),
        cost_estimate=LIGHT,
        name="unsort_half",
    )(where, perm, *blocks, *kept)


def fold_kernel(plan, where, factors, *refs):
    parts, group = plan.parts, plan.group
    terms = [ref[0].astype(F32) for ref in refs[:parts]]
    outs, kept = refs[-1 - group : -1], refs[-1]
    for r in range(parts):
        kept[0, r] = refs[r][0]
    for j in range(group):
        for which in range(2):
            total = None
            for r in range(parts):
                place = ((where[2] ^ j) * 2 + which) * parts + (where[1] ^ r)
                term = factors[place] * terms[r]
                total = term if total is None else total + term
            outs[j][which] = total.astype(LOW)


def fold(plan, where, blocks, after=(), cost=LIGHT):
    parts = plan.parts
    _, per, width = blocks[0].shape
    step = min(256, per)
    steps = per // step
    stack = pl.BlockSpec((1, parts, step, width), lambda c, k: (c, 0, k, 0))
    single = pl.BlockSpec((1, step, width), lambda c, k: (c, k, 0))
    out = pl.BlockSpec((2, step, width), lambda c, k: (0, c * steps + k, 0))
    return pl.pallas_call(
        functools.partial(fold_kernel, plan),
        grid=(2, steps),
        in_specs=[SCALARS, SCALARS] + [single] * parts + [LATER] * len(after),
        out_specs=[out] * plan.group + [stack],
        out_shape=[jax.ShapeDtypeStruct((2, 2 * per, width), LOW)] * plan.group
        + [jax.ShapeDtypeStruct((2, parts, per, width), LOW)],
        compiler_params=params(),
        cost_estimate=cost,
        name="fold_parts",
    )(where, jnp.asarray(plan.fold_table().reshape(-1)), *blocks, *after)


def turn_waves(plan, where, pairs, wave, turned, step):
    first = jnp.where(where[2] == 0, 1.0, 0.0).astype(F32)
    rest = 1.0 - first
    width = wave.shape[0]
    own = pairs[0].shape[1]
    rows = own * plan.group
    for j, pair in enumerate(pairs):
        for k in range(own // step):
            span = slice(k * step, (k + 1) * step)
            pw = dot(pair[0, span], wave[...])
            qw = dot(pair[1, span], wave[...])
            pc, ps, qc, qs = pw[:, :width], pw[:, width:], qw[:, :width], qw[:, width:]
            at = j * own + k * step
            turned[0, at : at + step] = (pc + rest * qs).astype(LOW)
            turned[0, rows + at : rows + at + step] = (rest * qc - ps).astype(LOW)
            turned[1, at : at + step] = (first * qc + rest * (pc - qs)).astype(LOW)
            turned[1, rows + at : rows + at + step] = (-first * qs - rest * (qc + ps)).astype(LOW)


def normed(resid, gain, shift):
    centered = resid - jnp.mean(resid, axis=-1, keepdims=True)
    inverse = lax.rsqrt(jnp.mean(centered * centered, axis=-1, keepdims=True) + epsilon)
    scaled = centered * inverse
    return scaled * gain + shift, scaled, inverse


def forward_kernel(plan, where, *refs):
    group, parts = plan.group, plan.parts
    pairs, refs = refs[:group], refs[group:]
    (wave, cos_rows, sin_rows, taken, b_in, vectors, *refs) = refs
    (w_in, w_out), refs, copies = split_weights(plan, where, refs)
    acts, (low_out, one_out, two_out, scales, hidden_out, slope_out, turned) = refs[:parts], refs[parts:]
    c, r = pl.program_id(0), pl.program_id(1)
    _, many, per, width = taken.shape
    rows = many * per

    @pl.when((c == 0) & (r == 0))
    def _():
        for copy in copies():
            copy.start()
        turn_waves(plan, where, pairs, wave, turned, min(256, pairs[0].shape[1]))
        for copy in copies():
            copy.wait()

    mixed = section(cos_rows, sin_rows, turned, c)
    b_out, gain_one, shift_one, gain_two, shift_two = (vectors[k : k + 1] for k in range(5))
    resid = taken[0].reshape(rows, width).astype(F32) + mixed
    normed_one, scaled_one, inverse_one = normed(resid, gain_one, shift_one)
    low = normed_one.astype(LOW)
    low_out[0] = low.reshape(many, per, width)
    one_out[0] = scaled_one.astype(LOW).reshape(many, per, width)
    branch = normed_one + b_out
    for h in range(parts):
        pre = dot(low, w_in[h]) + b_in[h : h + 1]
        square = pre * pre
        bend = jnp.tanh(pre * (GELU_C + (GELU_C * GELU_A) * square))
        half = 0.5 * pre
        hidden = (half + half * bend).astype(LOW)
        slope = 0.5 + 0.5 * bend + half * (1.0 - bend * bend) * (GELU_C + (3.0 * GELU_C * GELU_A) * square)
        hidden_out[0, :, h] = hidden.reshape(many, per, hidden.shape[1])
        slope_out[0, :, h] = slope.astype(LOW).reshape(many, per, hidden.shape[1])
        branch = branch + dot(hidden, w_out[h])
    normed_two, scaled_two, inverse_two = normed(branch, gain_two, shift_two)
    two_out[0] = scaled_two.astype(LOW).reshape(many, per, width)
    lanes = lax.broadcasted_iota(jnp.int32, (rows, 128), 1)
    scales[0] = jnp.where(lanes == 0, inverse_one, inverse_two).reshape(many, per, 128)
    act = normed_two.astype(LOW)
    for k in range(parts):

        @pl.when(r == k // many)
        def _(k=k):
            acts[k][0] = act[k % many * per : (k % many + 1) * per]


def section(cos_rows, sin_rows, turned, c):
    rows = cos_rows.shape[2]
    return dot(cos_rows[0], turned[c, :rows]) + dot(sin_rows[0], turned[c, rows:])


def weight_specs(plan, weights):
    return [LATER if plan.slabs else once(w.shape) for w in weights]


def weight_scratch(plan, weights):
    if not plan.slabs:
        return []
    chunks, slab, hid = weights[0].shape
    return [
        pltpu.VMEM((chunks, slab * len(weights), hid), LOW),
        pltpu.SemaphoreType.DMA((len(weights),)),
    ]


def slab_copies(plan, where, slabs, room, sems):
    slab = slabs[0].shape[1]
    for j, ref in enumerate(slabs):
        at = pl.multiple_of((where[4] ^ j) * slab, 16)
        yield pltpu.make_async_copy(ref, room.at[:, pl.ds(at, slab)], sems.at[j])


def split_weights(plan, where, refs):
    if plan.slabs:
        slabs, refs, room, sems = refs[: plan.dp], refs[plan.dp : -2], refs[-2], refs[-1]

        def copies():
            return slab_copies(plan, where, slabs, room, sems)

        return (room.at[: plan.parts], room.at[plan.parts :]), refs, copies
    return refs[:2], refs[2:], lambda: ()


def forward(plan, where, pairs, wave, tables, taken, b_in, vectors, weights):
    parts = plan.parts
    _, _, per, width = taken.shape
    rows = per * parts
    hid = b_in.shape[1]
    many = 1
    tile = pl.BlockSpec((1, many, per, width), lambda c, r: (c, r, 0, 0))
    wide = pl.BlockSpec((1, many, parts, per, hid), lambda c, r: (c, r, 0, 0, 0))
    low = jax.ShapeDtypeStruct((2, parts, per, width), LOW)
    big = jax.ShapeDtypeStruct((2, parts, parts, per, hid), LOW)
    return pl.pallas_call(
        functools.partial(forward_kernel, plan),
        grid=(2, parts // many),
        in_specs=[SCALARS]
        + [once(pairs[0].shape)] * plan.group
        + [
            once(wave.shape),
            pl.BlockSpec((1, many * per, rows), lambda c, r: (c, r, 0)),
            pl.BlockSpec((1, many * per, rows), lambda c, r: (c, r, 0)),
            tile,
            once(b_in.shape),
            once(vectors.shape),
        ]
        + weight_specs(plan, weights),
        out_specs=[pl.BlockSpec((1, per, width), lambda c, r: (c, 0, 0))] * parts
        + [tile, tile, tile, pl.BlockSpec((1, many, per, 128), lambda c, r: (c, r, 0, 0)), wide, wide],
        out_shape=[jax.ShapeDtypeStruct((2, per, width), LOW)] * parts
        + [low, low, low, jax.ShapeDtypeStruct((2, parts, per, 128), F32), big, big],
        scratch_shapes=[pltpu.VMEM((2, 2 * rows, width), LOW)] + weight_scratch(plan, weights),
        compiler_params=params(),
        cost_estimate=LIGHT,
        name="mix_forward",
    )(where, *pairs, wave, *tables, taken, b_in, vectors, *weights)


def norm_back(grad, scaled, inverse, gain):
    grad_scaled = grad * gain
    return inverse * (
        grad_scaled
        - jnp.mean(grad_scaled, axis=-1, keepdims=True)
        - scaled * jnp.mean(grad_scaled * scaled, axis=-1, keepdims=True)
    )


def column_sum(value):
    return jnp.sum(value, axis=0, keepdims=True)


def backward_kernel(plan, tiles, where, factors, *refs):
    parts, group = plan.parts, plan.group
    cotangents, refs = refs[:parts], refs[parts:]
    (two, scales_two, low, hidden, slope, one, scales_one, vectors, *refs) = refs
    (w_in, w_out), refs, copies = split_weights(plan, where, refs)
    (first_out, sums, bias, *refs) = refs
    folded, halves, refs = refs[:group], refs[group : group + 4], refs[group + 4 :]
    (grad_in, grad_out, cotangent, coming, coming_low, branch, total, leaving, rounded, *refs) = refs
    stages, sems = refs[:4], refs[4]
    step = pl.program_id(0)
    gain_one, gain_two = vectors[1:2], vectors[3:4]
    half = grad_in.shape[1] // 2

    def norm_two():
        r = lax.rem(step, parts)
        for k in range(parts):

            @pl.when(r == k)
            def _(k=k):
                cotangent[...] = cotangents[k][0]

    def stage_two():
        grad = cotangent[...].astype(F32)
        scaled = two[0, 0].astype(F32)
        second = norm_back(grad, scaled, scales_two[0, 0, :, 1:2], gain_two)
        second_low = second.astype(LOW)
        sums[2:3] += column_sum(grad * scaled)
        sums[3:4] += column_sum(grad)
        sums[4:5] += column_sum(second_low.astype(F32))
        coming[...] = second
        coming_low[...] = second_low

    def turn_over():
        leaving[...] = total[...]
        total[...] = coming[...]
        branch[...] = coming_low[...]

    def feed(last):
        low_turned = low[0, 0].T
        branch_turned = branch[...].T
        for h in range(parts):
            pre = (dot_nt(branch[...], w_out[h]) * slope[0, 0, h].astype(F32)).astype(LOW)
            bias[h : h + 1] += column_sum(pre.astype(F32))
            total[...] += dot_nt(pre, w_in[h])
            grads = (dot(low_turned, pre), dot(branch_turned, hidden[0, 0, h]))
            if not last:
                grad_in[h] += grads[0]
                grad_out[h] += grads[1]
                continue
            for k, (kept, grad) in enumerate(zip((grad_in, grad_out), grads)):
                grad = (kept[h] + grad).astype(LOW)
                stages[2 * k][h] = jnp.where(where[3] == 0, grad[:half], grad[half:])
                stages[2 * k + 1][h] = jnp.where(where[3] == 0, grad[half:], grad[:half])
            for k in range(4):
                pltpu.make_async_copy(stages[k].at[h], halves[k].at[h], sems.at[k, h]).start()

    def norm_one(valid):
        back = jnp.where(valid, leaving[...], 0.0)
        scaled = one[0, 0].astype(F32)
        first = norm_back(back, scaled, scales_one[0, 0, :, 0:1], gain_one)
        sums[0:1] += column_sum(back * scaled)
        sums[1:2] += column_sum(back)
        first_out[0, 0] = first
        rounded[lax.rem(jnp.maximum(step - 2, 0), parts)] = first.astype(LOW)

    def fold_all():
        for j in range(group):
            for which in range(2):
                value = None
                for r in range(parts):
                    place = ((where[2] ^ j) * 2 + which) * parts + (where[1] ^ r)
                    term = factors[place] * rounded[r].astype(F32)
                    value = term if value is None else value + term
                folded[j][which] = value.astype(LOW)

    @pl.when(step == 0)
    def _():
        for copy in copies():
            copy.start()
        sums[...] = jnp.zeros_like(sums)
        bias[...] = jnp.zeros_like(bias)
        grad_in[...] = jnp.zeros_like(grad_in)
        grad_out[...] = jnp.zeros_like(grad_out)

    @pl.when(step < tiles)
    def _():
        norm_two()

    @pl.when(step == 0)
    def _():
        stage_two()
        for copy in copies():
            copy.wait()

    @pl.when((step > 0) & (step < tiles))
    def _():
        turn_over()
        stage_two()
        feed(False)
        norm_one(step > 1)

    @pl.when(step == tiles)
    def _():
        turn_over()
        feed(True)
        norm_one(True)

    @pl.when(step == tiles + 1)
    def _():
        leaving[...] = total[...]
        norm_one(True)

    @pl.when((step > 1) & (lax.rem(step - 1, parts) == 0))
    def _():
        fold_all()

    @pl.when(step == tiles + 1)
    def _():
        for k in range(4):
            for h in range(parts):
                pltpu.make_async_copy(stages[k].at[h], halves[k].at[h], sems.at[k, h]).wait()


def backward(plan, where, cotangents, low, one, two, scales, hidden, slope, vectors, weights):
    parts, group = plan.parts, plan.group
    _, _, per, width = low.shape
    hid = hidden.shape[-1]
    tiles = 2 * parts

    def tile(lag, *rest):
        def place(s):
            at = jnp.clip(s - lag, 0, tiles - 1)
            return (at // parts, at % parts) + (0,) * len(rest)

        return pl.BlockSpec((1, 1, *rest), place)

    def class_of(lag):
        return lambda s: jnp.clip(s - lag, 0, tiles - 1) // parts

    half = jax.ShapeDtypeStruct((parts, width // 2, hid), LOW)
    return pl.pallas_call(
        functools.partial(backward_kernel, plan, tiles),
        grid=(tiles + 2,),
        in_specs=[SCALARS, SCALARS]
        + [pl.BlockSpec((1, per, width), lambda s: (class_of(0)(s), 0, 0))] * parts
        + [
            tile(0, per, width),
            tile(0, per, 128),
            tile(1, per, width),
            tile(1, parts, per, hid),
            tile(1, parts, per, hid),
            tile(2, per, width),
            tile(2, per, 128),
            once(vectors.shape),
        ]
        + weight_specs(plan, weights),
        out_specs=[tile(2, per, width), once((8, width)), once((parts, hid))]
        + [pl.BlockSpec((2, per, width), lambda s: (0, class_of(2)(s), 0))] * group
        + [LATER] * 4,
        out_shape=[
            jax.ShapeDtypeStruct((2, parts, per, width), F32),
            jax.ShapeDtypeStruct((8, width), F32),
            jax.ShapeDtypeStruct((parts, hid), F32),
        ]
        + [jax.ShapeDtypeStruct((2, 2 * per, width), LOW)] * group
        + [half] * 4,
        scratch_shapes=[
            pltpu.VMEM((parts, width, hid), F32),
            pltpu.VMEM((parts, width, hid), F32),
            pltpu.VMEM((per, width), LOW),
            pltpu.VMEM((per, width), F32),
            pltpu.VMEM((per, width), LOW),
            pltpu.VMEM((per, width), LOW),
            pltpu.VMEM((per, width), F32),
            pltpu.VMEM((per, width), F32),
            pltpu.VMEM((parts, per, width), LOW),
        ]
        + [pltpu.VMEM(half.shape, LOW)] * 4
        + [pltpu.SemaphoreType.DMA((4, parts))]
        + weight_scratch(plan, weights),
        compiler_params=params(),
        cost_estimate=LONG,
        name="feed_backward",
    )(
        where,
        jnp.asarray(plan.fold_table().reshape(-1)),
        *cotangents,
        two,
        scales,
        low,
        hidden,
        slope,
        one,
        scales,
        vectors,
        *weights,
    )


def mix_back_kernel(plan, where, *refs):
    group = plan.group
    pairs, (wave, cos_rows, sin_rows, first), outs, turned = (
        refs[:group],
        refs[group : group + 4],
        refs[-1 - group : -1],
        refs[-1],
    )
    c, r = pl.program_id(0), pl.program_id(1)
    _, many, per, width = first.shape

    @pl.when((c == 0) & (r == 0))
    def _():
        turn_waves(plan, where, pairs, wave, turned, min(256, pairs[0].shape[1]))

    total = first[0].reshape(many * per, width) + section(cos_rows, sin_rows, turned, c)
    total = total.astype(LOW)
    for k in range(group):

        @pl.when(r == k // many)
        def _(k=k):
            outs[k][0] = total[k % many * per : (k % many + 1) * per]


def mix_back(plan, where, pairs, wave, tables, first, half, after=(), cost=LIGHT):
    parts, group = plan.parts, plan.group
    _, _, per, width = first.shape
    rows = per * parts
    many = 2
    begin = half * group // many
    return pl.pallas_call(
        functools.partial(mix_back_kernel, plan),
        grid=(2, group // many),
        in_specs=[SCALARS]
        + [once(pairs[0].shape)] * group
        + [
            once(wave.shape),
            pl.BlockSpec((1, many * per, rows), lambda c, r: (c, begin + r, 0)),
            pl.BlockSpec((1, many * per, rows), lambda c, r: (c, begin + r, 0)),
            pl.BlockSpec((1, many, per, width), lambda c, r: (c, begin + r, 0, 0)),
        ]
        + [LATER] * len(after),
        out_specs=[pl.BlockSpec((1, per, width), lambda c, r: (c, 0, 0))] * group,
        out_shape=[jax.ShapeDtypeStruct((2, per, width), LOW)] * group,
        scratch_shapes=[pltpu.VMEM((2, 2 * rows, width), LOW)],
        compiler_params=params(),
        cost_estimate=cost,
        name="mix_backward",
    )(where, *pairs, wave, *tables, first, *after)


def add_split_kernel(bits, *refs):
    for k in range(2):
        one, two, keep, give = refs[2 * k], refs[2 * k + 1], refs[4 + 2 * k], refs[5 + 2 * k]
        total = (one[...].astype(F32) + two[...].astype(F32)).astype(LOW)
        half = keep.shape[1]
        low_half, high_half = total[:, :half], total[:, half:]
        keep[...] = jnp.where(bits[k] == 0, low_half, high_half)
        give[...] = jnp.where(bits[k] == 0, high_half, low_half)


def add_split(bits, pairs, cost):
    chunks, rows, hid = pairs[0][0].shape
    block = pl.BlockSpec((1, rows, hid), lambda h: (h, 0, 0))
    half = pl.BlockSpec((1, rows // 2, hid), lambda h: (h, 0, 0))
    outs = pl.pallas_call(
        add_split_kernel,
        grid=(chunks,),
        in_specs=[SCALARS] + [block] * 4,
        out_specs=[half] * 4,
        out_shape=[jax.ShapeDtypeStruct((chunks, rows // 2, hid), LOW)] * 4,
        compiler_params=params(),
        cost_estimate=cost,
        name="add_split",
    )(bits, *pairs[0], *pairs[1])
    return [outs[:2], outs[2:]]


def add_spread_kernel(order, *refs):
    for k in range(2):
        total = (refs[2 * k][...].astype(F32) + refs[2 * k + 1][...].astype(F32)).astype(LOW)
        for at, chunk in enumerate(order):
            refs[4 + chunk][k] = total[at]


def add_spread(order, pairs):
    chunks, rows, hid = pairs[0][0].shape
    block = pl.BlockSpec((chunks, rows, hid), lambda: (0, 0, 0))
    return pl.pallas_call(
        functools.partial(add_spread_kernel, order),
        in_specs=[block] * 4,
        out_specs=[pl.BlockSpec((2, rows, hid), lambda: (0, 0, 0))] * chunks,
        out_shape=[jax.ShapeDtypeStruct((2, rows, hid), LOW)] * chunks,
        compiler_params=params(),
        cost_estimate=LIGHT,
        name="add_spread",
    )(*pairs[0], *pairs[1])


def add_all_kernel(*refs):
    total = refs[0][...].astype(F32)
    for ref in refs[1:-1]:
        total = total + ref[...].astype(F32)
    refs[-1][...] = total.astype(LOW)


def add_all(values):
    block = pl.BlockSpec(values[0].shape, lambda: (0, 0, 0))
    return pl.pallas_call(
        add_all_kernel,
        in_specs=[block] * len(values),
        out_specs=block,
        out_shape=jax.ShapeDtypeStruct(values[0].shape, LOW),
        compiler_params=params(),
        cost_estimate=LIGHT,
        name="add_all",
    )(*values)


def finish_kernel(places, *refs):
    blocks, (grad_in, grad_out, rows) = refs[:-3], refs[-3:]
    slab = blocks[0].shape[1]
    for j, block in enumerate(blocks):
        for k, out in enumerate((grad_in, rows)):
            at = pl.multiple_of(places[k * len(blocks) + j] * slab, 8)
            out[pl.ds(at, slab)] = block[k].astype(F32)
    grad_out[...] = rows[...].T


def finish(places, blocks):
    _, slab, hid = blocks[0].shape
    width = slab * len(blocks)
    step = math.gcd(hid, 256)
    return pl.pallas_call(
        finish_kernel,
        grid=(hid // step,),
        in_specs=[SCALARS] + [pl.BlockSpec((2, slab, step), lambda h: (0, 0, h))] * len(blocks),
        out_specs=[
            pl.BlockSpec((width, step), lambda h: (0, h)),
            pl.BlockSpec((step, width), lambda h: (h, 0)),
        ],
        out_shape=[
            jax.ShapeDtypeStruct((width, hid), F32),
            jax.ShapeDtypeStruct((hid, width), F32),
        ],
        scratch_shapes=[pltpu.VMEM((width, step), F32)],
        compiler_params=params(),
        cost_estimate=LIGHT,
        name="finish_weights",
    )(places, *blocks)


def angle_pair(steps, modulus):
    angle = (2.0 * math.pi / modulus) * (steps % modulus).astype(F32)
    return jnp.cos(angle), jnp.sin(angle)


def product_tables(coarse, fine, modulus, shape):
    cos_a, sin_a = angle_pair(coarse, modulus)
    cos_b, sin_b = angle_pair(fine, modulus)
    cos = (cos_a * cos_b - sin_a * sin_b).astype(LOW)
    sin = (sin_a * cos_b + cos_a * sin_b).astype(LOW)
    return cos.reshape(shape), sin.reshape(shape)


def width_table(index):
    width = index.shape[0]
    coarse = jnp.arange(width // 32, dtype=jnp.int32) * 32
    fine = jnp.arange(32, dtype=jnp.int32)
    pair = product_tables(
        (coarse[:, None] * index)[:, None, :], (fine[:, None] * index)[None], width, (width, width)
    )
    return jnp.concatenate(pair, axis=1)


def section_table(plan, g, b, rows):
    parts, group = plan.parts, plan.group
    length, per = rows * parts, rows // parts
    classes = jnp.asarray(plan.pairs, jnp.int32)
    steps = jnp.arange(per, dtype=jnp.int32)
    mine = lax.dynamic_index_in_dim(classes, g, 0, keepdims=False)
    cols = jnp.concatenate(
        [
            (lax.dynamic_index_in_dim(classes, g ^ j, 0, keepdims=False)[:, None] + parts * steps).reshape(-1)
            for j in range(group)
        ]
    )
    fine = jnp.arange(32, dtype=jnp.int32)
    coarse = jnp.concatenate([per * (b ^ r) + 32 * jnp.arange(per // 32, dtype=jnp.int32) for r in range(parts)])
    first = ((parts * coarse + mine[:, None])[:, :, None] * cols)[:, :, None, :]
    second = (parts * fine[:, None] * cols)[None, None]
    return product_tables(first, second, length, (2, rows, rows))


def body(plan, tokens, w_in, b_in, w_out, b_out, gain_one, shift_one, gain_two, shift_two, out_grad):
    seqs, rows, width = tokens.shape
    parts, group = plan.parts, plan.group
    hid = w_in.shape[1]
    d = lax.axis_index("dp")
    t = lax.axis_index("tensor")
    g = (t % plan.span) * 2 + d % 2
    b = (t // plan.span) % seqs * group + g
    where = jnp.stack([t, b, g, d % 2, d]).astype(jnp.int32)

    def permute(value, perm):
        return lax.ppermute(value, BOTH, perm)

    def tie(values, *after):
        return lax.optimization_barrier((*values, *after))[: len(values)]

    def over_pairs(own):
        blocks = {0: own}
        for j in range(2, plan.dp, 2):
            blocks[j] = permute(own, plan.xor_perm(j, 0))
        for j in range(0, plan.dp, 2):
            blocks[j + 1] = permute(blocks[j], plan.xor_perm(1, 0))
        return [blocks[j] for j in range(plan.dp)]

    z_bits = [1 << k for k in range(parts.bit_length() - 1)]
    slab_in, slab_out = width // plan.dp, hid // plan.dp
    flat_in = slab_in * hid // width
    packed = jnp.concatenate(
        [
            lax.dynamic_slice_in_dim(w_in, d * slab_in, slab_in, 0).reshape(flat_in, width),
            lax.dynamic_slice_in_dim(w_out, d * slab_out, slab_out, 0),
            jnp.pad(b_in[None], ((0, 15), (0, width - hid))),
        ]
    )
    sorted_tokens = sort_rows(plan, where, tokens)
    slabs, z_order = packed[None], [0]
    for bit in reversed(z_bits):
        z_order += [other ^ bit for other in z_order]
        slabs = jnp.concatenate([slabs, permute(slabs, plan.xor_perm(0, bit))])
        if bit == z_bits[-1]:
            slabs, *sorted_tokens = tie([slabs, *sorted_tokens])
    taken_blocks = [permute(block, plan.out_perm(r)) for r, block in enumerate(sorted_tokens)]

    bias_in = slabs[:, flat_in + slab_out, :hid].astype(F32)
    slabs_in = slabs[:, :flat_in].reshape(parts, slab_in, hid)
    slabs_out = slabs[:, flat_in : flat_in + slab_out]
    plan.slabs = slabs_in.shape == slabs_out.shape and slab_in % 16 == 0
    if plan.slabs:
        weights = over_pairs(tie([jnp.concatenate([slabs_in, slabs_out])], taken_blocks[0])[0])
    else:
        weights = [lax.all_gather(value, "dp", axis=1, tiled=True) for value in (slabs_in, slabs_out)]

    vectors = jnp.stack([b_out, gain_one, shift_one, gain_two, shift_two])
    late_g, late_b, index = tie([g, b, jnp.arange(width, dtype=jnp.int32)], taken_blocks[0])
    wave = width_table(index)
    tables = section_table(plan, late_g, late_b, rows)

    def send_back(blocks):
        return [permute(block, plan.back_perm(r)) for r, block in enumerate(blocks)]

    def exchange(folded):
        return [folded[0]] + [permute(folded[j], plan.group_perm(j)) for j in range(1, group)]

    sorted_grad = sort_rows(plan, where, out_grad, taken_blocks[:1])
    *folded, taken = fold(
        plan, where, taken_blocks, (wave, *tables, bias_in, vectors, sorted_grad[0], *weights[1:2]), LONG
    )
    sorted_grad = tie(sorted_grad, *taken_blocks)
    cotangents = [permute(block, plan.out_perm(r)) for r, block in enumerate(sorted_grad)]

    outs = forward(plan, where, exchange(folded), wave, tables, taken, bias_in, vectors, weights)
    acts, saved = send_back(outs[:parts]), outs[parts:]

    first, sums, bias, *rest = backward(plan, where, cotangents, *saved, vectors, weights)
    folded, halves = rest[:group], rest[group:]

    bits = [1 << k for k in range(plan.dp.bit_length() - 1)]
    orders = (bits, bits[:1] + bits[:0:-1])

    def bits_of(step):
        return jnp.stack([(d // order[step]) % 2 for order in orders]).astype(jnp.int32)

    def swap(pairs, step):
        return [
            (keep, permute(give, plan.xor_perm(order[step], 0)))
            for (keep, give), order in zip(pairs, orders)
        ]

    def tie_pairs(pairs, *after):
        flat = tie([x for pair in pairs for x in pair], *after)
        return [flat[:2], flat[2:]]

    def tree(values):
        while len(values) > 1:
            values = [one + two for one, two in zip(values[::2], values[1::2])]
        return values[0]

    folded = tie(folded, *acts)
    exchanged = exchange(folded)
    grad_blocks = list(mix_back(plan, where, exchanged, wave, tables, first, 0))
    halves = tie(halves, *exchanged)
    pairs = tie_pairs(swap([halves[:2], halves[2:]], 0), grad_blocks[0])
    halves = add_split(bits_of(1), pairs, LIGHT)
    flat = [x for pair in halves for x in pair]
    grad_blocks += mix_back(plan, where, exchanged, wave, tables, first, 1, flat, LONG)

    returned = []

    def give_back(r, *after):
        block = tie([grad_blocks[r]], *after)[0] if after else grad_blocks[r]
        returned.append(permute(block, plan.back_perm(r)))

    for r in range(group):
        give_back(r)
    activations = unsort_rows(plan, where, tie(acts, grad_blocks[-1]))
    for k in range(1, len(bits) - 1):
        halves = add_split(bits_of(k + 1), tie_pairs(swap(halves, k), activations), LIGHT)
    for r in range(group, parts - 1):
        give_back(r, *returned[:group], activations)
    input_grad = unsort_half(plan, where, returned[:group], 0)
    small = tie([jnp.concatenate([sums[:5], bias.reshape(-1, width)])], input_grad)[0]
    for bit in bits:
        small = small + permute(small, plan.xor_perm(bit, 0))
    pairs = tie_pairs(swap(halves, len(bits) - 1), activations, small, *returned)
    chunks = add_spread(z_order, pairs)

    values = [chunks[0]] + [permute(chunks[k], plan.xor_perm(0, k)) for k in range(1, parts)]
    flat_sums, bias = small[:5].reshape(-1), small[5:].reshape(parts, hid)
    pads = [jnp.concatenate([flat_sums, bias[z_order.index(k)]]) for k in range(parts)]
    pads = tie(pads, chunks[0])
    got = [pads[0]] + [permute(pads[k], plan.xor_perm(0, k)) for k in range(1, parts)]
    small = tree(got)
    give_back(parts - 1, *values)
    total = add_all(values)
    blocks = {0: total}
    for j in range(2, plan.dp, 2):
        blocks[j] = permute(total, plan.xor_perm(j, 0))
    input_grad = unsort_half(plan, where, returned[group:], 1, input_grad)
    blocks[plan.dp - 2] = tie([blocks[plan.dp - 2]], input_grad)[0]
    for j in range(0, plan.dp, 2):
        blocks[j + 1] = permute(blocks[j], plan.xor_perm(1, 0))
    blocks = [blocks[j] for j in range(plan.dp)]
    places = [
        sum((((d ^ j) // bit) % 2) * (plan.dp >> k + 1) for k, bit in enumerate(order))
        for order in orders
        for j in range(plan.dp)
    ]
    grad_w_in, grad_w_out = finish(jnp.stack(places).astype(jnp.int32), blocks)
    return (
        activations,
        input_grad,
        grad_w_in,
        small[5 * width :],
        grad_w_out,
        *(small[k * width : (k + 1) * width] for k in (4, 0, 1, 2, 3)),
    )


def solution(mesh):
    def shards(tokens, *rest):
        return body(Plan(mesh, tokens.shape[0]), tokens, *rest)

    rows = P("dp", "tensor", None)
    return jax.shard_map(
        shards,
        mesh=mesh,
        in_specs=(rows, P(None, "tensor"), P("tensor"), P("tensor", None), P(), P(), P(), P(), P(), rows),
        out_specs=(rows, rows, P(None, "tensor"), P("tensor"), P("tensor", None), P(), P(), P(), P(), P()),
        check_vma=False,
    )
```
